512 devices in a mesh: depth: 64 (over x, z), rays: 8 (over y, core).
Axes of the slice: x: 4, y: 4, z: 16, core: 2. Of those that a mesh axis runs over, the one named last changes fastest.
Arguments:
- encoded: bfloat16 [64, 4, 4096, 256], P('depth', None, 'rays'), may hold values from -6 to 6
- deltas: float32 [64, 4, 4096], P('depth', None, 'rays'), may hold values from 0.00390625 to 0.03125
- w_in: bfloat16 [64, 256, 512], P('depth'), may hold values from -0.375 to 0.375
- w_mid: bfloat16 [64, 512, 512], P('depth'), may hold values from -0.25 to 0.25
- w_sigma: bfloat16 [64, 512], P('depth'), may hold values from -0.25 to 0.25
- order: int32 [8, 64], P('rays'), may hold values from 0 to 63, each once within a row
- target: bfloat16 [4096, 512], P('rays'), may hold values from -3 to 3
Outputs:
- grad_in: float32 [64, 256, 512], P('depth', 'rays')
- grad_mid: float32 [64, 512, 512], P('depth', 'rays')
- grad_sigma: float32 [64, 512], P('depth', 'rays')
- loss: float32 [], replicated
The draws below stay inside these ranges and needn't reach their ends.
Inputs may be any that keep to these rules, and one draw needn't show every extreme that they name: Each row of order lists every region once.
All inputs are finite; a program needn't handle non-finite values.
Results may differ from the reference program's by a relative error of at most 0.015.
Values may be sent and summed in bfloat16 or wider, within the bound.
A program may use at most 64 MiB of HBM per device.

```python
import math
import jax
import jax.numpy as jnp
from jax import lax

E = 256
H = 512
F = 512
S = 4
R_DEV = 512
REGIONS = 64
GROUPS = 8
RAYS = 4096


def strengthened(values, stream_key, source, target, shards_of, factor):
    def block_of(dim):
        return (jnp.arange(values.shape[dim]) // (values.shape[dim] // shards_of)).reshape((-1,) + (1,) * (values.ndim - 1 - dim))

    near = jax.random.permutation(stream_key, shards_of)[block_of(target)]
    far = (block_of(target) + shards_of // 2) % shards_of
    return jnp.where((block_of(source) == near) | (block_of(source) == far), factor * values, values)


def level_of(key, shape, split, low, high):
    gain, own = 1.0, jax.random.fold_in(key, 6)
    for axis_at, parts in split:
        heights = jnp.exp(jax.random.uniform(jax.random.fold_in(own, axis_at), (parts,), jnp.float32, low / len(split), high / len(split)))
        gain = gain * jnp.repeat(heights, shape[axis_at] // parts).reshape([-1 if axis == axis_at else 1 for axis in range(len(shape))])
    return gain


def noise(stream_key, shape, width, most, split=(), kind=jnp.bfloat16):
    loudness = level_of(stream_key, shape, split, -0.22, 0.18) if split else 1.0
    array = jax.random.normal(stream_key, shape, jnp.float32) * width * loudness
    return jnp.minimum(jnp.maximum(array, -most), most).astype(kind)


def noise_with(own_key, dims, width, bound, cuts, heavy, kind=jnp.bfloat16):
    values = width * jax.random.normal(own_key, dims, jnp.float32)
    if cuts:
        values = values * level_of(own_key, dims, cuts, -0.22, 0.18)
    return jnp.clip(strengthened(values, jax.random.fold_in(own_key, 3), *heavy), -bound, bound).astype(kind)


def setup_inputs(seed: int = 0) -> dict:
    keys = jax.random.split(jax.random.key(seed), 8)
    return {
        "encoded": noise_with(keys[0], (REGIONS, S, RAYS, E), 1.0, 6.0, ((0, 64), (2, 8)), (2, 3, 8, 2.0)),
        "deltas": jnp.clip(jnp.exp(math.log(0.03125) - 2.0794415 * jax.random.uniform(keys[1], (REGIONS, S, RAYS), jnp.float32) ** level_of(keys[1], (REGIONS, S, RAYS), ((0, 64), (2, 8)), -0.2, 0.2)), 0.00390625, 0.03125),
        "w_in": noise(keys[2], (REGIONS, E, H), E ** -0.5, 0.375, ((0, 64),)),
        "w_mid": noise(keys[3], (REGIONS, H, F), H ** -0.5, 0.25, ((0, 64),)),
        "w_sigma": noise(keys[4], (REGIONS, H), H ** -0.5, 0.25, ((0, 64),)),
        "order": jax.vmap(lambda own: jax.random.permutation(own, REGIONS))(jax.random.split(keys[5], GROUPS)).reshape((GROUPS, REGIONS)).astype(jnp.int32),
        "target": noise(keys[6], (RAYS, F), 0.5, 3.0, ((0, 8),)),
    }


def local_fields(x, w1, w2, ws, delta):
    rows = x.reshape(-1, x.shape[-1])
    hidden = jnp.maximum(jnp.dot(rows, w1, preferred_element_type=jnp.float32), 0.0)
    hidden_b = hidden.astype(jnp.bfloat16)
    feat = jnp.dot(hidden_b, w2, preferred_element_type=jnp.float32)
    logit = jnp.dot(hidden_b, ws, preferred_element_type=jnp.float32)
    tau = jax.nn.softplus(logit).reshape(delta.shape) * delta
    excl = jnp.cumsum(tau, axis=0) - tau
    weight = jnp.exp(-excl) * (1.0 - jnp.exp(-tau))
    return rows, hidden, hidden_b, feat, logit, tau, excl, weight


def region_forward(args):
    x, w1, w2, ws, delta = args
    rows, hidden, hidden_b, feat, logit, tau, excl, weight = local_fields(x, w1, w2, ws, delta)
    feat3 = feat.reshape(S, -1, F)
    segment = jnp.sum(weight[:, :, None] * feat3, axis=0)
    return segment, jnp.sum(tau, axis=0)


def region_backward(args, dcolor):
    x, w1, w2, ws, delta, trans, gtau = args
    rows, hidden, hidden_b, feat, logit, tau, excl, weight = local_fields(x, w1, w2, ws, delta)
    dseg = trans[:, None] * dcolor
    feat3 = feat.reshape(S, -1, F)
    dfeat = (weight[:, :, None] * dseg[None]).astype(jnp.bfloat16)
    vsum = jnp.sum(feat3 * dseg[None], axis=2)
    wv = weight * vsum
    dtau = jnp.exp(-(excl + tau)) * vsum - (jnp.sum(wv, axis=0)[None] - jnp.cumsum(wv, axis=0)) + gtau[None]
    dz = (dtau * delta).reshape(-1) * jax.nn.sigmoid(logit)
    dfeat2 = dfeat.reshape(-1, F)
    dhb = jnp.dot(dfeat2, w2.T, preferred_element_type=jnp.float32) + dz[:, None] * ws.astype(jnp.float32)[None]
    dpre = jnp.where(hidden > 0, dhb, 0.0).astype(jnp.bfloat16)
    x4 = rows.reshape(S, GROUPS, R_DEV, E).astype(jnp.float32)
    p4 = dpre.reshape(S, GROUPS, R_DEV, H).astype(jnp.float32)
    h4 = hidden_b.reshape(S, GROUPS, R_DEV, H).astype(jnp.float32)
    f4 = dfeat2.reshape(S, GROUPS, R_DEV, F).astype(jnp.float32)
    z4 = dz.reshape(S, GROUPS, R_DEV)
    part_in = jnp.einsum('sgre,sgrh->geh', x4, p4, precision=lax.Precision.HIGHEST)
    part_mid = jnp.einsum('sgrh,sgrf->ghf', h4, f4, precision=lax.Precision.HIGHEST)
    part_sig = jnp.einsum('sgrh,sgr->gh', h4, z4, precision=lax.Precision.HIGHEST)

    def settle(part):
        return jnp.sum(lax.optimization_barrier(part.astype(jnp.bfloat16)).astype(jnp.float32), axis=0)

    return settle(part_in), settle(part_mid), settle(part_sig)


def reference(encoded, deltas, w_in, w_mid, w_sigma, order, target):
    segment, depth_tau = lax.map(region_forward, (encoded, w_in, w_mid, w_sigma, deltas))
    positions = jnp.arange(REGIONS, dtype=jnp.int32)
    onehot = order[:, :, None] == positions[None, None, :]
    rank = jnp.sum(jnp.where(onehot, positions[None, :, None], 0), axis=1).astype(jnp.int32)
    before = (rank[:, None, :] < rank[:, :, None]).astype(jnp.float32)
    tau_g = depth_tau.reshape(REGIONS, GROUPS, R_DEV)
    prefix = jnp.einsum('grs,sgi->rgi', before, tau_g, precision=lax.Precision.HIGHEST).reshape(REGIONS, RAYS)
    trans = jnp.exp(-prefix)
    color = jnp.sum(trans[:, :, None] * segment, axis=0)
    err = color - target.astype(jnp.float32)
    loss = jnp.sum(err * err) / (RAYS * F)
    dcolor = lax.optimization_barrier(err.astype(jnp.bfloat16)).astype(jnp.float32)
    qsum = jnp.sum(segment * dcolor[None], axis=2)
    contrib = (trans * qsum).reshape(REGIONS, GROUPS, R_DEV)
    gtau = -jnp.einsum('gsr,sgi->rgi', before, contrib, precision=lax.Precision.HIGHEST).reshape(REGIONS, RAYS)
    grad_in, grad_mid, grad_sigma = lax.map(lambda a: region_backward(a, dcolor), (encoded, w_in, w_mid, w_sigma, deltas, trans, gtau))
    return grad_in, grad_mid, grad_sigma, loss
```

```python
import functools

import jax
import jax.numpy as jnp
from jax import lax
from jax.experimental import pallas as pl
from jax.experimental.pallas import tpu as pltpu
from jax.sharding import PartitionSpec as P

MESH = pl.DeviceIdType.MESH
XS, ZS, YS = 4, 16, 4
S = 4
Q = 128
E, H, F = 256, 512, 512
FB = 256
RB = 16
bf16, f32 = jnp.bfloat16, jnp.float32


def coords():
    d = lax.axis_index("depth")
    r = lax.axis_index("rays")
    return d // ZS, d % ZS, r // 2, r % 2


def device(x, z, y, c):
    return (x * ZS + z, y * 2 + c)


def remote(src, dst, send, recv, to):
    return pltpu.make_async_remote_copy(
        src_ref=src, dst_ref=dst, send_sem=send, recv_sem=recv, device_id=to, device_id_type=MESH
    )


def column(row):
    return jnp.transpose(jnp.broadcast_to(row, (Q, Q)))


def wide(a, n):
    return jnp.concatenate([a] * n, axis=1)


def stack(rows):
    at = lax.broadcasted_iota(jnp.int32, (8, Q), 0)
    out = jnp.zeros((8, Q), f32)
    for i, row in rows:
        out = jnp.where(at == i, row, out)
    return out


def far_first(i):
    k = (i + 1) // 2
    return ZS // 2 + k * (2 * (i % 2) - 1)


def kernel(
    enc, dlt, win_h, wmid_h, wsig, order, tgt,
    gi, gm, gs, loss,
    xb, win, wmid, tb, wsr, hid, hbt, xt, wrep, comp,
    sg_out, sg_in, tx_out, tx_in, tz, tr_out, tr_in,
    zs, zr, dc, uz, gx_out, gx_in,
    dsg, gg, vc, pmf, cm_out, cm_in, ym_own, ym_out, ym_in,
    pif, ci_out, ci_in, yi_own, yi_out, yi_in, sb, sc_in, sy_out, sy_in, dp,
    s_enc, s_w, sg_s, sg_r, tx_s, tx_r, tz_s, tz_r, tr_s, tr_r, zr_s, zr_r, za_s, za_r,
    xa_s, xa_r, uz_s, uz_r, gx_s, gx_r, c_s, c_r, ym_s, ym_r, yi_s, yi_r, sy_s, sy_r,
):
    x, z, y, c = coords()
    xd = lambda k: device((x + k) % XS, z, y, c)
    zd = lambda k: device(x, (z + k) % ZS, y, c)
    yd = lambda k: device(x, z, (y + k) % YS, c)
    other = device(x, z, y, 1 - c)
    zj, zh = z // 2, z % 2
    block = pl.ds(pl.multiple_of(zj * RB, RB), RB)

    def rays_of(d):
        return pl.multiple_of(((x + d) % XS) * Q, Q)

    load_in = pltpu.make_async_copy(win_h.at[0], win, s_w.at[0])
    load_in.start()

    def enc_copy(d):
        return pltpu.make_async_copy(enc.at[0, :, pl.ds(rays_of(d), Q), :], xb.at[d], s_enc.at[d])

    enc_copy(0).start()
    load_mid = pltpu.make_async_copy(wmid_h.at[0], wmid, s_w.at[1])
    load_mid.start()
    for d in range(1, XS):
        enc_copy(d).start()
    load_t = pltpu.make_async_copy(
        tgt.at[pl.ds(pl.multiple_of(x * Q + zj * RB, RB), RB), pl.ds(pl.multiple_of(zh * FB, FB), FB)], tb, s_w.at[2]
    )
    load_t.start()

    barrier = pltpu.get_barrier_semaphore()
    for k in range(1, XS):
        pl.semaphore_signal(barrier, inc=1, device_id=xd(k), device_id_type=MESH)
        pl.semaphore_signal(barrier, inc=1, device_id=yd(k), device_id_type=MESH)
    pl.semaphore_signal(barrier, inc=1, device_id=other, device_id_type=MESH)

    def greet(i, _):
        pl.semaphore_signal(barrier, inc=1, device_id=zd(far_first(i)), device_id_type=MESH)
        return 0

    lax.fori_loop(0, ZS - 1, greet, 0)

    eye = lax.broadcasted_iota(jnp.int32, (Q, Q), 0) == lax.broadcasted_iota(jnp.int32, (Q, Q), 1)
    sigma = wsig[...].astype(f32)
    for t in range(H // Q):
        wsr[t * Q:(t + 1) * Q, :] = column(sigma[:, t * Q:(t + 1) * Q]).astype(bf16)
    load_in.wait()

    def forward(d, _):
        enc_copy(d).wait()
        hp = jnp.dot(xb[d].reshape(S * Q, E), win[...], preferred_element_type=f32)
        h = jnp.maximum(hp, 0.0).astype(bf16)
        hid[d] = h
        lg = jnp.dot(h, wsr[...], preferred_element_type=f32)
        excl = jnp.zeros((1, Q), f32)
        hb = jnp.zeros((Q, H), f32)
        for k in range(S):
            logit = jnp.sum(jnp.where(eye, lg[k * Q:(k + 1) * Q], 0.0), axis=0, keepdims=True)
            delta = dlt[0, k:k + 1, pl.ds(rays_of(d), Q)]
            tau = (jnp.maximum(logit, 0.0) + jnp.log1p(jnp.exp(-jnp.abs(logit)))) * delta
            weight = jnp.exp(-excl) * (1.0 - jnp.exp(-tau))
            excl = excl + tau
            comp[d, k:k + 1, :] = weight
            comp[d, S + k:S + k + 1, :] = jnp.exp(-excl)
            comp[d, 2 * S + k:2 * S + k + 1, :] = delta / (1.0 + jnp.exp(-logit))
            wk = column(weight)
            wrep[d, k] = wk
            hb = hb + wide(wk, H // Q) * h[k * Q:(k + 1) * Q].astype(f32)
        tx_out[d] = stack([(0, excl)])
        hbt[d] = jnp.transpose(hb).astype(bf16)
        seg = jnp.dot(hb.astype(bf16), wmid[...], preferred_element_type=f32).astype(bf16)
        sg_out[d, 0] = seg[:, :FB]
        sg_out[d, 1] = seg[:, FB:]
        return 0

    load_mid.wait()
    lax.fori_loop(0, XS, forward, 0)

    pl.semaphore_wait(barrier, 2 * (XS - 1) + 1 + ZS - 1)

    def tx(k):
        return remote(tx_out.at[k], tx_in.at[k], tx_s.at[k], tx_r.at[k], xd(k))

    def sg(k, h):
        return remote(sg_out.at[k, h], sg_in.at[k, h], sg_s.at[k, h], sg_r.at[k, h], xd(k))

    for k in (2, 1, 3):
        tx(k).start()
    for h in range(2):
        for k in (2, 1, 3):
            sg(k, h).start()
    for k in (1, 3, 2):
        tx(k).wait_recv()
    tz[0] = stack([(0, tx_out[0, 0:1, :])] + [(k, tx_in[k, 0:1, :]) for k in range(1, XS)])

    def tz_copy(k):
        return remote(tz.at[0], tz.at[k], tz_s.at[k], tz_r.at[k], zd(k))

    lax.fori_loop(0, ZS - 1, lambda i, _: (tz_copy(far_first(i)).start(), 0)[1], 0)

    def turn(i, _):
        d, k = i // S, i % S
        t = jnp.transpose(xb[d, k].astype(f32)).astype(bf16)
        xt[d, :, pl.ds(pl.multiple_of(k * Q, Q), Q)] = t
        return 0

    lax.fori_loop(0, XS * S, turn, 0)
    row = lax.broadcasted_iota(jnp.int32, (ZS * 8, XS * ZS), 0)
    place = lax.broadcasted_iota(jnp.int32, (ZS * 8, XS * ZS), 1)
    region = ((x + XS - row % 8) % XS) * ZS + (z + ZS - row // 8) % ZS
    at = (region == order[...]) & (row % 8 < XS)
    rank = jnp.sum(jnp.where(at, place, 0).astype(f32), axis=1, keepdims=True)
    real = lax.broadcasted_iota(jnp.int32, (ZS * 8, 1), 0) % 8 < XS

    lax.fori_loop(1, ZS, lambda k, _: (tz_copy(k).wait_recv(), 0)[1], 0)
    taus = tz[...].reshape(ZS * 8, Q)
    trans = []
    for d in range(XS):
        front = (rank < rank[d:d + 1]) & real
        trans.append(jnp.exp(-jnp.sum(jnp.where(front, taus, 0.0), axis=0, keepdims=True)))
        tr_out[d] = stack([(0, trans[d])])

    def tr(k):
        return remote(tr_out.at[k], tr_in.at[k], tr_s.at[k], tr_r.at[k], xd(XS - k))

    for k in (2, 1, 3):
        tr(k).start()

    shade = [column(trans[d]) for d in range(XS)]
    for h in range(2):
        total = wide(shade[0], FB // Q) * sg_out[0, h].astype(f32)
        for k in range(1, XS):
            sg(k, h).wait_recv()
            total = total + wide(shade[k], FB // Q) * sg_in[k, h].astype(f32)
        zs[h] = total.astype(bf16)

    def zr_copy(k):
        to = (z + k) % ZS
        src = zs.at[to % 2, pl.ds(pl.multiple_of((to // 2) * RB, RB), RB), :]
        return remote(src, zr.at[k], zr_s.at[k], zr_r.at[k], zd(k))

    lax.fori_loop(0, ZS - 1, lambda i, _: (zr_copy(far_first(i)).start(), 0)[1], 0)
    zr[0] = zs[zh, block, :]
    load_t.wait()
    lax.fori_loop(1, ZS, lambda k, _: (zr_copy(k).wait_recv(), 0)[1], 0)
    color = jnp.sum(zr[...].astype(f32), axis=0)
    err = color - tb[...].astype(f32)
    square = jnp.sum(err * err, axis=0, keepdims=True)
    square = square[:, :Q] + square[:, Q:]
    dc[0, zh, block, :] = err.astype(bf16)

    def za_copy(k):
        ref = dc.at[0, zh, block, :]
        return remote(ref, ref, za_s.at[k], za_r.at[k], zd(k))

    lax.fori_loop(0, ZS - 1, lambda i, _: (za_copy(far_first(i)).start(), 0)[1], 0)

    def za_wait(k, _):
        at_z = (z + ZS - k) % ZS
        ref = dc.at[0, at_z % 2, pl.ds(pl.multiple_of((at_z // 2) * RB, RB), RB), :]
        remote(ref, ref, za_s.at[k], za_r.at[k], zd(k)).wait_recv()
        return 0

    lax.fori_loop(1, ZS, za_wait, 0)

    def xa(k, h):
        return remote(dc.at[0, h], dc.at[k, h], xa_s.at[k, h], xa_r.at[k, h], xd(XS - k))

    for h in range(2):
        for k in (2, 1, 3):
            xa(k, h).start()

    terms = []
    for d in range(XS):
        seg = sg_out if d == 0 else sg_in
        part = jnp.zeros((Q, Q), f32)
        for h in range(2):
            prod = seg[d, h].astype(f32) * dc[0, h].astype(f32)
            part = part + prod[:, :Q] + prod[:, Q:]
        terms.append(trans[d] * jnp.sum(jnp.transpose(part), axis=0, keepdims=True))
    uz[0] = stack(list(enumerate(terms)) + [(XS, square)])

    def uz_copy(k):
        return remote(uz.at[0], uz.at[k], uz_s.at[k], uz_r.at[k], zd(k))

    lax.fori_loop(0, ZS - 1, lambda i, _: (uz_copy(far_first(i)).start(), 0)[1], 0)

    for k in range(1, XS):
        tr(k).wait_recv()
    tr_in[0] = tr_out[0]

    def backward(d, _):
        @pl.when(d > 0)
        def _():
            for h in range(2):
                xa(d, h).wait_recv()

        t = wide(column(tr_in[d, 0:1, :]), F // Q)
        grad = jnp.concatenate([dc[d, 0], dc[d, 1]], axis=1).astype(f32)
        grad = (t * grad).astype(bf16)
        dsg[d] = grad
        g = lax.dot_general(grad, wmid[...], (((1,), (1,)), ((), ())), preferred_element_type=f32)
        gg[d] = g
        for k in range(S):
            prod = hid[d, k * Q:(k + 1) * Q, :].astype(f32) * g
            part = prod[:, :Q] + prod[:, Q:2 * Q] + prod[:, 2 * Q:3 * Q] + prod[:, 3 * Q:]
            vc[d, k:k + 1, :] = jnp.sum(jnp.transpose(part), axis=0, keepdims=True)
        return 0

    lax.fori_loop(0, XS, backward, 0)
    mid = jnp.dot(hbt[0], dsg[0], preferred_element_type=f32)
    for d in range(1, XS):
        mid = mid + jnp.dot(hbt[d], dsg[d], preferred_element_type=f32)
    pmf[...] = mid.reshape(YS, 2, H // (2 * YS), F)
    cm_out[...] = pmf[:, pl.ds(1 - c, 1)].reshape(YS, H // (2 * YS), F).astype(bf16)
    cm = remote(cm_out, cm_in, c_s.at[0], c_r.at[0], other)
    cm.start()

    lax.fori_loop(1, ZS, lambda k, _: (uz_copy(k).wait_recv(), 0)[1], 0)
    us = uz[...].reshape(ZS * 8, Q)
    squares = jnp.zeros((1, Q), f32)
    for k in range(ZS):
        squares = squares + uz[(z + ZS - k) % ZS, XS:XS + 1, :]
    for d in range(XS):
        behind = (rank > rank[d:d + 1]) & real
        back = -jnp.sum(jnp.where(behind, us, 0.0), axis=0, keepdims=True)
        gx_out[d] = stack([(0, back), (1, squares)])

    def gx(k):
        return remote(gx_out.at[k], gx_in.at[k], gx_s.at[k], gx_r.at[k], xd(XS - k))

    for k in (2, 1, 3):
        gx(k).start()
    gx_in[0] = gx_out[0]

    cm.wait_recv()
    own = pmf[:, pl.ds(c, 1)].reshape(YS, H // (2 * YS), F) + cm_in[...].astype(f32)
    ym_own[...] = own
    ym_out[...] = own.astype(bf16)

    def ym(k):
        return remote(ym_out.at[(y + k) % YS], ym_in.at[k], ym_s.at[k], ym_r.at[k], yd(k))

    for k in (2, 1, 3):
        ym(k).start()

    for k in (1, 3, 2):
        gx(k).wait_recv()
    pif[...] = jnp.zeros_like(pif)
    lines = sigma

    def finish(d, sig):
        gtau = gx_in[d, 0:1, :]
        later = jnp.zeros((1, Q), f32)
        g = gg[d]
        for k in reversed(range(S)):
            v = vc[d, k:k + 1, :]
            dtau = comp[d, S + k:S + k + 1, :] * v - later + gtau
            later = later + comp[d, k:k + 1, :] * v
            dz = wide(column(dtau * comp[d, 2 * S + k:2 * S + k + 1, :]), H // Q)
            h = hid[d, k * Q:(k + 1) * Q, :].astype(f32)
            pre = wide(wrep[d, k], H // Q) * g + dz * lines
            dp[k * Q:(k + 1) * Q, :] = jnp.where(h > 0.0, pre, 0.0).astype(bf16)
            sig = sig + jnp.sum((h * dz).reshape(Q // 8, 8, H), axis=0)
        pif[...] += jnp.dot(xt[d], dp[...], preferred_element_type=f32).reshape(pif.shape)
        return sig

    sig = lax.fori_loop(0, XS, finish, jnp.zeros((8, H), f32))
    sig = jnp.sum(sig, axis=0, keepdims=True)
    ci_out[...] = pif[:, pl.ds(1 - c, 1)].reshape(YS, E // (2 * YS), H).astype(bf16)
    ci = remote(ci_out, ci_in, c_s.at[1], c_r.at[1], other)
    ci.start()
    squares = jnp.zeros((1, Q), f32)
    for q in range(XS):
        squares = squares + gx_in[(q + XS - x) % XS, 1:2, :]
    sb[...] = stack([(t, sig[:, t * Q:(t + 1) * Q]) for t in range(H // Q)] + [(H // Q, squares)])
    sc = remote(sb, sc_in, c_s.at[2], c_r.at[2], other)
    sc.start()
    ci.wait_recv()
    own = pif[:, pl.ds(c, 1)].reshape(YS, E // (2 * YS), H) + ci_in[...].astype(f32)
    yi_own[...] = own
    yi_out[...] = own.astype(bf16)

    def yi(k):
        return remote(yi_out.at[(y + k) % YS], yi_in.at[k], yi_s.at[k], yi_r.at[k], yd(k))

    for k in (2, 1, 3):
        yi(k).start()
    sc.wait_recv()
    sy_out[...] = sb[...] + sc_in[...]
    sy_in[0] = sy_out[...]

    def sy(k):
        return remote(sy_out, sy_in.at[k], sy_s.at[k], sy_r.at[k], yd(k))

    for k in (2, 1, 3):
        sy(k).start()

    for k in range(1, YS):
        ym(k).wait_recv()
    total = ym_own[y]
    for k in range(1, YS):
        total = total + ym_in[k].astype(f32)
    gm[0] = total
    for k in range(1, YS):
        yi(k).wait_recv()
    total = yi_own[y]
    for k in range(1, YS):
        total = total + yi_in[k].astype(f32)
    gi[0] = total
    for k in range(1, YS):
        sy(k).wait_recv()
    total = jnp.zeros((8, Q), f32)
    for k in range(YS):
        total = total + sy_in[(y + YS - k) % YS]
    line = jnp.sum(jnp.where(lax.broadcasted_iota(jnp.int32, (8, Q), 0) == y, total, 0.0), axis=0, keepdims=True)
    gs[...] = jnp.where(c == 0, line[:, :Q // 2], line[:, Q // 2:])
    loss[0, 0] = jnp.sum(total[H // Q:H // Q + 1]) / (XS * Q * 2 * YS * F)

    for k in range(1, XS):
        tx(k).wait_send()
        tr(k).wait_send()
        gx(k).wait_send()
        ym(k).wait_send()
        yi(k).wait_send()
        sy(k).wait_send()
        for h in range(2):
            sg(k, h).wait_send()
            xa(k, h).wait_send()
    cm.wait_send()
    ci.wait_send()
    sc.wait_send()

    def sent(k, _):
        tz_copy(k).wait_send()
        zr_copy(k).wait_send()
        za_copy(k).wait_send()
        uz_copy(k).wait_send()
        return 0

    lax.fori_loop(1, ZS, sent, 0)


def body(encoded, deltas, w_in, w_mid, w_sigma, order, target):
    vm = pl.BlockSpec(memory_space=pltpu.VMEM)
    hbm = pl.BlockSpec(memory_space=pl.ANY)
    dma = pltpu.SemaphoreType.DMA
    v = pltpu.VMEM
    hm, hi = H // (2 * YS), E // (2 * YS)
    scratch = [
        v((XS, S, Q, E), bf16), v((E, H), bf16), v((H, F), bf16), v((RB, FB), bf16), v((H, Q), bf16),
        v((XS, S * Q, H), bf16), v((XS, H, Q), bf16), v((XS, E, S * Q), bf16), v((XS, S, Q, Q), f32), v((XS, 16, Q), f32),
        v((XS, 2, Q, FB), bf16), v((XS, 2, Q, FB), bf16), v((XS, 8, Q), f32), v((XS, 8, Q), f32), v((ZS, 8, Q), f32),
        v((XS, 8, Q), f32), v((XS, 8, Q), f32),
        v((2, Q, FB), bf16), v((ZS, RB, FB), bf16), v((XS, 2, Q, FB), bf16), v((ZS, 8, Q), f32),
        v((XS, 8, Q), f32), v((XS, 8, Q), f32),
        v((XS, Q, F), bf16), v((XS, Q, H), f32), v((XS, 8, Q), f32), v((YS, 2, hm, F), f32),
        v((YS, hm, F), bf16), v((YS, hm, F), bf16), v((YS, hm, F), f32), v((YS, hm, F), bf16), v((YS, hm, F), bf16),
        v((YS, 2, hi, H), f32),
        v((YS, hi, H), bf16), v((YS, hi, H), bf16), v((YS, hi, H), f32), v((YS, hi, H), bf16), v((YS, hi, H), bf16),
        v((8, Q), f32), v((8, Q), f32), v((8, Q), f32), v((YS, 8, Q), f32), v((S * Q, H), bf16),
        dma((XS,)), dma((3,)), dma((XS, 2)), dma((XS, 2)), dma((XS,)), dma((XS,)), dma((ZS,)), dma((ZS,)),
        dma((XS,)), dma((XS,)), dma((ZS,)), dma((ZS,)), dma((ZS,)), dma((ZS,)),
        dma((XS, 2)), dma((XS, 2)), dma((ZS,)), dma((ZS,)), dma((XS,)), dma((XS,)), dma((3,)), dma((3,)),
        dma((YS,)), dma((YS,)), dma((YS,)), dma((YS,)), dma((YS,)), dma((YS,)),
    ]
    grad_in, grad_mid, grad_sigma, loss = pl.pallas_call(
        kernel,
        out_shape=(
            jax.ShapeDtypeStruct((1, hi, H), f32),
            jax.ShapeDtypeStruct((1, hm, F), f32),
            jax.ShapeDtypeStruct((1, hm), f32),
            jax.ShapeDtypeStruct((1, 1), f32),
        ),
        in_specs=[hbm, vm, hbm, hbm, vm, vm, hbm],
        out_specs=(vm, vm, vm, pl.BlockSpec(memory_space=pltpu.SMEM)),
        scratch_shapes=scratch,
        compiler_params=pltpu.CompilerParams(collective_id=0, has_side_effects=True, vmem_limit_bytes=48 << 20),
        name="field_step",
    )(encoded, deltas, w_in, w_mid, w_sigma, order, target)
    return grad_in, grad_mid, grad_sigma, loss[0, 0]


def solution(mesh):
    in_specs = (
        P("depth", None, "rays", None),
        P("depth", None, "rays"),
        P("depth", None, None),
        P("depth", None, None),
        P("depth", None),
        P("rays", None),
        P("rays", None),
    )
    out_specs = (P("depth", "rays", None), P("depth", "rays", None), P("depth", "rays"), P())
    return jax.shard_map(body, mesh=mesh, in_specs=in_specs, out_specs=out_specs, check_vma=False)
```

```python
import functools

import jax
import jax.numpy as jnp
from jax import lax
from jax.experimental import pallas as pl
from jax.experimental.pallas import tpu as pltpu
from jax.sharding import PartitionSpec as P

MESH = pl.DeviceIdType.MESH
XS, ZS, YS = 4, 16, 4
ZP = ZS // 2
G = 2 * XS
S = 4
Q = 128
E, H, F = 256, 512, 512
FB = 256
RB = 16
bf16, f32 = jnp.bfloat16, jnp.float32


def coords():
    d = lax.axis_index("depth")
    r = lax.axis_index("rays")
    return d // ZS, d % ZS, r // 2, r % 2


def device(x, z, y, c):
    return (x * ZS + z, y * 2 + c)


def remote(src, dst, send, recv, to):
    return pltpu.make_async_remote_copy(
        src_ref=src, dst_ref=dst, send_sem=send, recv_sem=recv, device_id=to, device_id_type=MESH
    )


def column(row):
    return jnp.transpose(jnp.broadcast_to(row, (Q, Q)))


def wide(a, n):
    return jnp.concatenate([a] * n, axis=1)


def stack(rows):
    at = lax.broadcasted_iota(jnp.int32, (8, Q), 0)
    out = jnp.zeros((8, Q), f32)
    for i, row in rows:
        out = jnp.where(at == i, row, out)
    return out


def far_first(i, n):
    k = (i + 1) // 2
    return n // 2 + k * (2 * (i % 2) - 1)


def each(first, last, f):
    def step(i, _):
        f(i)
        return 0

    lax.fori_loop(first, last, step, 0)


def kernel(
    enc, dlt_h, win_h, wmid_h, wsig_h, order_h, tgt,
    gi, gm, gs, loss,
    xb, win, wmid, tb, wsr, hid, hbt, xt, wrep, comp,
    sg_out, sg_in, tx_out, tx_in, tz, tr_out, tr_in,
    zs, zr, dc, uz, gx_out, gx_in,
    dsg, gg, vc, pmf, cm_out, cm_in, ym_own, ym_out, ym_in,
    pif, ci_out, ci_in, yi_own, yi_out, yi_in, sb, sc_in, sy_out, sy_in, dp, dlt, wsig, order,
    s_enc, s_w, sg_s, sg_r, tx_s, tx_r, tz_s, tz_r, tr_s, tr_r, zr_s, zr_r, za_s, za_r,
    xa_s, xa_r, uz_s, uz_r, gx_s, gx_r, c_s, c_r, ym_s, ym_r, yi_s, yi_r, sy_s, sy_r,
):
    x, z, y, c = coords()
    xd = lambda k: device((x + k) % XS, z, y, c)
    zd = lambda k: device(x, (z + 2 * k) % ZS, y, c)
    yd = lambda k: device(x, z, (y + k) % YS, c)
    other = device(x, z, y, 1 - c)
    zj, zh = z // 2, z % 2
    pair = lambda e: z + e * (1 - 2 * zh)
    ahead = lambda m: device((x + m // 2) % XS, pair(m % 2), y, c)
    back = lambda m: device((x + XS - m // 2) % XS, pair(m % 2), y, c)
    block = pl.ds(pl.multiple_of(zj * RB, RB), RB)

    def rays_of(d):
        return pl.multiple_of(((x + d) % XS) * Q, Q)

    load_s = pltpu.make_async_copy(wsig_h, wsig, s_w.at[3])
    load_s.start()
    load_d = pltpu.make_async_copy(dlt_h, dlt, s_w.at[4])
    load_d.start()
    load_o = pltpu.make_async_copy(order_h, order, s_w.at[5])
    load_o.start()
    load_in = pltpu.make_async_copy(win_h.at[0], win, s_w.at[0])
    load_in.start()

    def enc_copy(d):
        return pltpu.make_async_copy(enc.at[0, :, pl.ds(rays_of(d), Q), :], xb.at[d], s_enc.at[d])

    enc_copy(0).start()
    load_mid = pltpu.make_async_copy(wmid_h.at[0], wmid, s_w.at[1])
    load_mid.start()
    for d in range(1, XS):
        enc_copy(d).start()
    load_t = pltpu.make_async_copy(
        tgt.at[pl.ds(pl.multiple_of(x * Q + zj * RB, RB), RB), pl.ds(pl.multiple_of(zh * FB, FB), FB)], tb, s_w.at[2]
    )
    load_t.start()

    barrier = pltpu.get_barrier_semaphore()
    for k in range(1, YS):
        pl.semaphore_signal(barrier, inc=1, device_id=yd(k), device_id_type=MESH)
    pl.semaphore_signal(barrier, inc=1, device_id=other, device_id_type=MESH)
    each(0, ZP - 1, lambda i: pl.semaphore_signal(barrier, inc=1, device_id=zd(far_first(i, ZP)), device_id_type=MESH))
    each(1, G, lambda m: pl.semaphore_signal(barrier, inc=1, device_id=ahead(m), device_id_type=MESH))

    eye = lax.broadcasted_iota(jnp.int32, (Q, Q), 0) == lax.broadcasted_iota(jnp.int32, (Q, Q), 1)
    load_s.wait()
    sigma = wsig[...].astype(f32)
    for t in range(H // Q):
        wsr[t * Q:(t + 1) * Q, :] = column(sigma[:, t * Q:(t + 1) * Q]).astype(bf16)
    load_in.wait()

    def forward(d, _):
        enc_copy(d).wait()
        hp = jnp.dot(xb[d].reshape(S * Q, E), win[...], preferred_element_type=f32)
        h = jnp.maximum(hp, 0.0).astype(bf16)
        hid[d] = h
        lg = jnp.dot(h, wsr[...], preferred_element_type=f32)
        excl = jnp.zeros((1, Q), f32)
        hb = jnp.zeros((Q, H), f32)
        for k in range(S):
            logit = jnp.sum(jnp.where(eye, lg[k * Q:(k + 1) * Q], 0.0), axis=0, keepdims=True)
            delta = dlt[0, k:k + 1, pl.ds(rays_of(d), Q)]
            tau = (jnp.maximum(logit, 0.0) + jnp.log1p(jnp.exp(-jnp.abs(logit)))) * delta
            weight = jnp.exp(-excl) * (1.0 - jnp.exp(-tau))
            excl = excl + tau
            comp[d, k:k + 1, :] = weight
            comp[d, S + k:S + k + 1, :] = jnp.exp(-excl)
            comp[d, 2 * S + k:2 * S + k + 1, :] = delta / (1.0 + jnp.exp(-logit))
            wk = column(weight)
            wrep[d, k] = wk
            hb = hb + wide(wk, H // Q) * h[k * Q:(k + 1) * Q].astype(f32)
        tx_out[d] = stack([(0, excl)])
        hbt[d] = jnp.transpose(hb).astype(bf16)
        seg = jnp.dot(hb.astype(bf16), wmid[...], preferred_element_type=f32).astype(bf16)
        sg_out[d, 0] = seg[:, :FB]
        sg_out[d, 1] = seg[:, FB:]
        return 0

    load_mid.wait()
    load_d.wait()
    lax.fori_loop(0, XS, forward, 0)

    pl.semaphore_wait(barrier, YS - 1 + 1 + ZP - 1 + G - 1)

    def tx(m):
        return remote(tx_out.at[m // 2], tx_in.at[m], tx_s.at[m], tx_r.at[m], ahead(m))

    def sg(m):
        return remote(sg_out.at[m // 2, (zh + m) % 2], sg_in.at[m], sg_s.at[m], sg_r.at[m], ahead(m))

    each(1, G, lambda m: tx(m).start())
    each(1, G, lambda m: sg(m).start())
    tx_in[0] = tx_out[0]
    sg_in[0] = sg_out[0, zh]
    each(1, G, lambda m: tx(m).wait_recv())
    tz[0] = stack([(m, tx_in[m, 0:1, :]) for m in range(G)])

    def tz_copy(k):
        return remote(tz.at[0], tz.at[k], tz_s.at[k], tz_r.at[k], zd(k))

    each(0, ZP - 1, lambda i: tz_copy(far_first(i, ZP)).start())

    def turn(i, _):
        d, k = i // S, i % S
        t = jnp.transpose(xb[d, k].astype(f32)).astype(bf16)
        xt[d, :, pl.ds(pl.multiple_of(k * Q, Q), Q)] = t
        return 0

    lax.fori_loop(0, XS * S, turn, 0)
    load_o.wait()
    row = lax.broadcasted_iota(jnp.int32, (XS * ZS, XS * ZS), 0)
    place = lax.broadcasted_iota(jnp.int32, (XS * ZS, XS * ZS), 1)
    at_z = (z + ZS - 2 * (row // G)) % ZS + (row % 2) * (1 - 2 * zh)
    region = ((x + XS - row % G // 2) % XS) * ZS + at_z
    rank = jnp.sum(jnp.where(region == order[...], place, 0).astype(f32), axis=1, keepdims=True)

    each(1, ZP, lambda k: tz_copy(k).wait_recv())
    taus = tz[...].reshape(XS * ZS, Q)
    trans = []
    for m in range(G):
        front = rank < rank[m:m + 1]
        trans.append(jnp.exp(-jnp.sum(jnp.where(front, taus, 0.0), axis=0, keepdims=True)))
    for d in range(XS):
        tr_out[d] = stack([(0, trans[2 * d])])

    def tr(k):
        return remote(tr_out.at[k], tr_in.at[k], tr_s.at[k], tr_r.at[k], back(2 * k))

    for k in (2, 1, 3):
        tr(k).start()

    total = jnp.zeros((Q, FB), f32)
    for m in range(G):
        if m:
            sg(m).wait_recv()
        total = total + wide(column(trans[m]), FB // Q) * sg_in[m].astype(f32)
    zs[...] = total.astype(bf16)

    def zr_copy(k):
        src = zs.at[pl.ds(pl.multiple_of(((zj + k) % ZP) * RB, RB), RB), :]
        return remote(src, zr.at[k], zr_s.at[k], zr_r.at[k], zd(k))

    each(0, ZP - 1, lambda i: zr_copy(far_first(i, ZP)).start())
    zr[0] = zs[block, :]
    load_t.wait()
    each(1, ZP, lambda k: zr_copy(k).wait_recv())
    color = jnp.sum(zr[...].astype(f32), axis=0)
    err = color - tb[...].astype(f32)
    square = jnp.sum(err * err, axis=0, keepdims=True)
    square = square[:, :Q] + square[:, Q:]
    dc[0, zh, block, :] = err.astype(bf16)

    def za_copy(k):
        ref = dc.at[0, zh, block, :]
        return remote(ref, ref, za_s.at[k], za_r.at[k], zd(k))

    each(0, ZP - 1, lambda i: za_copy(far_first(i, ZP)).start())

    def za_wait(k):
        ref = dc.at[0, zh, pl.ds(pl.multiple_of(((zj + ZP - k) % ZP) * RB, RB), RB), :]
        remote(ref, ref, za_s.at[k], za_r.at[k], zd(k)).wait_recv()

    each(1, ZP, za_wait)

    def xa(m):
        return remote(dc.at[0, zh], dc.at[m // 2, zh], xa_s.at[m], xa_r.at[m], back(m))

    def xa_wait(m):
        ref = dc.at[m // 2, (zh + m) % 2]
        remote(ref, ref, xa_s.at[m], xa_r.at[m], back(m)).wait_recv()

    each(1, G, lambda m: xa(m).start())

    grad = dc[0, zh].astype(f32)
    terms = []
    for m in range(G):
        prod = sg_in[m].astype(f32) * grad
        part = jnp.transpose(prod[:, :Q] + prod[:, Q:])
        terms.append(trans[m] * jnp.sum(part, axis=0, keepdims=True))
    uz[0, :G, :] = stack(list(enumerate(terms)))
    uz[0, G:, :] = stack([(0, square)])

    def uz_copy(k):
        return remote(uz.at[0], uz.at[k], uz_s.at[k], uz_r.at[k], zd(k))

    each(0, ZP - 1, lambda i: uz_copy(far_first(i, ZP)).start())

    for k in range(1, XS):
        tr(k).wait_recv()
    tr_in[0] = tr_out[0]

    def backward(d, _):
        @pl.when(d > 0)
        def _():
            xa_wait(2 * d)

        xa_wait(2 * d + 1)

        t = wide(column(tr_in[d, 0:1, :]), F // Q)
        grad = jnp.concatenate([dc[d, 0], dc[d, 1]], axis=1).astype(f32)
        grad = (t * grad).astype(bf16)
        dsg[d] = grad
        g = lax.dot_general(grad, wmid[...], (((1,), (1,)), ((), ())), preferred_element_type=f32)
        gg[d] = g
        for k in range(S):
            prod = hid[d, k * Q:(k + 1) * Q, :].astype(f32) * g
            part = prod[:, :Q] + prod[:, Q:2 * Q] + prod[:, 2 * Q:3 * Q] + prod[:, 3 * Q:]
            vc[d, k:k + 1, :] = jnp.sum(jnp.transpose(part), axis=0, keepdims=True)
        return 0

    lax.fori_loop(0, XS, backward, 0)
    mid = jnp.dot(hbt[0], dsg[0], preferred_element_type=f32)
    for d in range(1, XS):
        mid = mid + jnp.dot(hbt[d], dsg[d], preferred_element_type=f32)
    pmf[...] = mid.reshape(YS, 2, H // (2 * YS), F)
    cm_out[...] = pmf[:, pl.ds(1 - c, 1)].reshape(YS, H // (2 * YS), F).astype(bf16)
    cm = remote(cm_out, cm_in, c_s.at[0], c_r.at[0], other)
    cm.start()

    each(1, ZP, lambda k: uz_copy(k).wait_recv())
    us = uz[:, :G, :].reshape(XS * ZS, Q)
    squares = jnp.zeros((1, Q), f32)
    for k in range(ZP):
        squares = squares + uz[(zj + ZP - k) % ZP, G:G + 1, :]
    for m in range(G):
        behind = rank > rank[m:m + 1]
        gx_out[m] = stack([(0, -jnp.sum(jnp.where(behind, us, 0.0), axis=0, keepdims=True)), (1, squares)])

    def gx(m):
        return remote(gx_out.at[m], gx_in.at[m], gx_s.at[m], gx_r.at[m], back(m))

    each(1, G, lambda m: gx(m).start())
    gx_in[0] = gx_out[0]

    cm.wait_recv()
    own = pmf[:, pl.ds(c, 1)].reshape(YS, H // (2 * YS), F) + cm_in[...].astype(f32)
    ym_own[...] = own
    ym_out[...] = own.astype(bf16)

    def ym(k):
        return remote(ym_out.at[(y + k) % YS], ym_in.at[k], ym_s.at[k], ym_r.at[k], yd(k))

    for k in (2, 1, 3):
        ym(k).start()

    each(1, G, lambda m: gx(m).wait_recv())
    pif[...] = jnp.zeros_like(pif)
    lines = sigma

    def finish(d, sig):
        gtau = gx_in[2 * d, 0:1, :] + gx_in[2 * d + 1, 0:1, :]
        later = jnp.zeros((1, Q), f32)
        g = gg[d]
        for k in reversed(range(S)):
            v = vc[d, k:k + 1, :]
            dtau = comp[d, S + k:S + k + 1, :] * v - later + gtau
            later = later + comp[d, k:k + 1, :] * v
            dz = wide(column(dtau * comp[d, 2 * S + k:2 * S + k + 1, :]), H // Q)
            h = hid[d, k * Q:(k + 1) * Q, :].astype(f32)
            pre = wide(wrep[d, k], H // Q) * g + dz * lines
            dp[k * Q:(k + 1) * Q, :] = jnp.where(h > 0.0, pre, 0.0).astype(bf16)
            sig = sig + jnp.sum((h * dz).reshape(Q // 8, 8, H), axis=0)
        pif[...] += jnp.dot(xt[d], dp[...], preferred_element_type=f32).reshape(pif.shape)
        return sig

    sig = lax.fori_loop(0, XS, finish, jnp.zeros((8, H), f32))
    sig = jnp.sum(sig, axis=0, keepdims=True)
    ci_out[...] = pif[:, pl.ds(1 - c, 1)].reshape(YS, E // (2 * YS), H).astype(bf16)
    ci = remote(ci_out, ci_in, c_s.at[1], c_r.at[1], other)
    ci.start()
    squares = jnp.zeros((1, Q), f32)
    for q in range(XS):
        for h in range(2):
            squares = squares + gx_in[2 * ((q + XS - x) % XS) + (h + zh) % 2, 1:2, :]
    sb[...] = stack([(t, sig[:, t * Q:(t + 1) * Q]) for t in range(H // Q)] + [(H // Q, squares)])
    sc = remote(sb, sc_in, c_s.at[2], c_r.at[2], other)
    sc.start()
    ci.wait_recv()
    own = pif[:, pl.ds(c, 1)].reshape(YS, E // (2 * YS), H) + ci_in[...].astype(f32)
    yi_own[...] = own
    yi_out[...] = own.astype(bf16)

    def yi(k):
        return remote(yi_out.at[(y + k) % YS], yi_in.at[k], yi_s.at[k], yi_r.at[k], yd(k))

    for k in (2, 1, 3):
        yi(k).start()
    sc.wait_recv()
    sy_out[...] = sb[...] + sc_in[...]
    sy_in[0] = sy_out[...]

    def sy(k):
        return remote(sy_out, sy_in.at[k], sy_s.at[k], sy_r.at[k], yd(k))

    for k in (2, 1, 3):
        sy(k).start()

    for k in range(1, YS):
        ym(k).wait_recv()
    total = ym_own[y]
    for k in range(1, YS):
        total = total + ym_in[k].astype(f32)
    gm[0] = total
    for k in range(1, YS):
        yi(k).wait_recv()
    total = yi_own[y]
    for k in range(1, YS):
        total = total + yi_in[k].astype(f32)
    gi[0] = total
    for k in range(1, YS):
        sy(k).wait_recv()
    total = jnp.zeros((8, Q), f32)
    for k in range(YS):
        total = total + sy_in[(y + YS - k) % YS]
    line = jnp.sum(jnp.where(lax.broadcasted_iota(jnp.int32, (8, Q), 0) == y, total, 0.0), axis=0, keepdims=True)
    gs[...] = jnp.where(c == 0, line[:, :Q // 2], line[:, Q // 2:])
    loss[0, 0] = jnp.sum(total[H // Q:H // Q + 1]) / (XS * Q * 2 * YS * F)

    for k in range(1, XS):
        tr(k).wait_send()
        ym(k).wait_send()
        yi(k).wait_send()
        sy(k).wait_send()
    cm.wait_send()
    ci.wait_send()
    sc.wait_send()

    def sent_group(m):
        tx(m).wait_send()
        sg(m).wait_send()
        xa(m).wait_send()
        gx(m).wait_send()

    each(1, G, sent_group)

    def sent_z(k):
        tz_copy(k).wait_send()
        zr_copy(k).wait_send()
        za_copy(k).wait_send()
        uz_copy(k).wait_send()

    each(1, ZP, sent_z)


def settle(gi, gm, gs, loss, gi_o, gm_o, gs_o, loss_o):
    gi_o[...] = gi[...]
    gm_o[...] = gm[...]
    gs_o[...] = gs[...]
    loss_o[0, 0] = loss[0, 0]


def body(encoded, deltas, w_in, w_mid, w_sigma, order, target):
    vm = pl.BlockSpec(memory_space=pltpu.VMEM)
    hbm = pl.BlockSpec(memory_space=pl.ANY)
    dma = pltpu.SemaphoreType.DMA
    v = pltpu.VMEM
    hm, hi = H // (2 * YS), E // (2 * YS)
    scratch = [
        v((XS, S, Q, E), bf16), v((E, H), bf16), v((H, F), bf16), v((RB, FB), bf16), v((H, Q), bf16),
        v((XS, S * Q, H), bf16), v((XS, H, Q), bf16), v((XS, E, S * Q), bf16), v((XS, S, Q, Q), f32), v((XS, 16, Q), f32),
        v((XS, 2, Q, FB), bf16), v((G, Q, FB), bf16), v((XS, 8, Q), f32), v((G, 8, Q), f32), v((ZP, 8, Q), f32),
        v((XS, 8, Q), f32), v((XS, 8, Q), f32),
        v((Q, FB), bf16), v((ZP, RB, FB), bf16), v((XS, 2, Q, FB), bf16), v((ZP, 16, Q), f32),
        v((G, 8, Q), f32), v((G, 8, Q), f32),
        v((XS, Q, F), bf16), v((XS, Q, H), f32), v((XS, 8, Q), f32), v((YS, 2, hm, F), f32),
        v((YS, hm, F), bf16), v((YS, hm, F), bf16), v((YS, hm, F), f32), v((YS, hm, F), bf16), v((YS, hm, F), bf16),
        v((YS, 2, hi, H), f32),
        v((YS, hi, H), bf16), v((YS, hi, H), bf16), v((YS, hi, H), f32), v((YS, hi, H), bf16), v((YS, hi, H), bf16),
        v((8, Q), f32), v((8, Q), f32), v((8, Q), f32), v((YS, 8, Q), f32), v((S * Q, H), bf16),
        v((1, S, XS * Q), f32), v((1, H), bf16), v((1, XS * ZS), jnp.int32),
        dma((XS,)), dma((6,)), dma((G,)), dma((G,)), dma((G,)), dma((G,)), dma((ZP,)), dma((ZP,)),
        dma((XS,)), dma((XS,)), dma((ZP,)), dma((ZP,)), dma((ZP,)), dma((ZP,)),
        dma((G,)), dma((G,)), dma((ZP,)), dma((ZP,)), dma((G,)), dma((G,)), dma((3,)), dma((3,)),
        dma((YS,)), dma((YS,)), dma((YS,)), dma((YS,)), dma((YS,)), dma((YS,)),
    ]
    grad_in, grad_mid, grad_sigma, loss = pl.pallas_call(
        kernel,
        out_shape=(
            jax.ShapeDtypeStruct((1, hi, H), f32),
            jax.ShapeDtypeStruct((1, hm, F), f32),
            jax.ShapeDtypeStruct((1, hm), f32),
            jax.ShapeDtypeStruct((1, 1), f32),
        ),
        in_specs=[hbm] * 7,
        out_specs=(vm, vm, vm, pl.BlockSpec(memory_space=pltpu.SMEM)),
        scratch_shapes=scratch,
        compiler_params=pltpu.CompilerParams(collective_id=0, has_side_effects=True, vmem_limit_bytes=60 << 20),
        name="field_step",
    )(encoded, deltas, w_in, w_mid, w_sigma, order, target)
    smem = pl.BlockSpec(memory_space=pltpu.SMEM)
    grad_in, grad_mid, grad_sigma, loss = pl.pallas_call(
        settle,
        out_shape=tuple(jax.ShapeDtypeStruct(a.shape, a.dtype) for a in (grad_in, grad_mid, grad_sigma, loss)),
        in_specs=[vm] * 3 + [smem],
        out_specs=(vm, vm, vm, smem),
        compiler_params=pltpu.CompilerParams(vmem_limit_bytes=60 << 20),
        name="settle",
    )(grad_in, grad_mid, grad_sigma, loss)
    return grad_in, grad_mid, grad_sigma, loss[0, 0]


def solution(mesh):
    in_specs = (
        P("depth", None, "rays", None),
        P("depth", None, "rays"),
        P("depth", None, None),
        P("depth", None, None),
        P("depth", None),
        P("rays", None),
        P("rays", None),
    )
    out_specs = (P("depth", "rays", None), P("depth", "rays", None), P("depth", "rays"), P())
    return jax.shard_map(body, mesh=mesh, in_specs=in_specs, out_specs=out_specs, check_vma=False)
```

```python
import functools

import jax
import jax.numpy as jnp
from jax import lax
from jax.experimental import pallas as pl
from jax.experimental.pallas import tpu as pltpu
from jax.sharding import PartitionSpec as P

MESH = pl.DeviceIdType.MESH
XS, ZS, YS = 4, 16, 4
ZP = ZS // 2
G = 2 * XS
S = 4
Q = 128
E, H, F = 256, 512, 512
FB = 256
RB = 16
bf16, f32 = jnp.bfloat16, jnp.float32


def coords():
    d = lax.axis_index("depth")
    r = lax.axis_index("rays")
    return d // ZS, d % ZS, r // 2, r % 2


def device(x, z, y, c):
    return (x * ZS + z, y * 2 + c)


def remote(src, dst, send, recv, to):
    return pltpu.make_async_remote_copy(
        src_ref=src, dst_ref=dst, send_sem=send, recv_sem=recv, device_id=to, device_id_type=MESH
    )


def column(row):
    return jnp.transpose(jnp.broadcast_to(row, (Q, Q)))


def wide(a, n):
    return jnp.concatenate([a] * n, axis=1)


def stack(rows):
    at = lax.broadcasted_iota(jnp.int32, (8, Q), 0)
    out = jnp.zeros((8, Q), f32)
    for i, row in rows:
        out = jnp.where(at == i, row, out)
    return out


def far_first(i, n):
    k = (i + 1) // 2
    return n // 2 + k * (2 * (i % 2) - 1)


def each(first, last, f):
    for i in range(first, last):
        f(i)


def kernel(
    enc, dlt_h, win_h, wmid_h, wsig_h, order_h, tgt,
    gi_o, gm_o, gs_o, loss,
    gi, gm, gs, xb, win, wmid, tb, wsr, hid, hbt, xt, wrep, comp,
    sg_out, sg_in, tx_out, tx_in, tz, tr_out, tr_in,
    zs, zr, dc, uz, gx_out, gx_in,
    dsg, gg, vc, pmf, cm_out, cm_in, ym_own, ym_out, ym_in,
    pif, ci_out, ci_in, yi_own, yi_out, yi_in, sb, sc_in, sy_out, sy_in, dp, dlt, wsig, order,
    s_enc, s_w, sg_s, sg_r, tx_s, tx_r, tz_s, tz_r, tr_s, tr_r, zr_s, zr_r, za_s, za_r,
    xa_s, xa_r, uz_s, uz_r, gx_s, gx_r, c_s, c_r, ym_s, ym_r, yi_s, yi_r, sy_s, sy_r,
):
    x, z, y, c = coords()
    xd = lambda k: device((x + k) % XS, z, y, c)
    zd = lambda k: device(x, (z + 2 * k) % ZS, y, c)
    yd = lambda k: device(x, z, (y + k) % YS, c)
    other = device(x, z, y, 1 - c)
    zj, zh = z // 2, z % 2
    pair = lambda e: z + e * (1 - 2 * zh)
    ahead = lambda m: device((x + m // 2) % XS, pair(m % 2), y, c)
    back = lambda m: device((x + XS - m // 2) % XS, pair(m % 2), y, c)
    block = pl.ds(pl.multiple_of(zj * RB, RB), RB)

    def rays_of(d):
        return pl.multiple_of(((x + d) % XS) * Q, Q)

    load_s = pltpu.make_async_copy(wsig_h, wsig, s_w.at[3])
    load_s.start()
    load_d = pltpu.make_async_copy(dlt_h, dlt, s_w.at[4])
    load_d.start()
    load_o = pltpu.make_async_copy(order_h, order, s_w.at[5])
    load_o.start()
    load_in = pltpu.make_async_copy(win_h.at[0], win, s_w.at[0])
    load_in.start()

    def rows_of(d):
        return pl.ds(d * Q if isinstance(d, int) else pl.multiple_of(d * Q, Q), Q)

    def enc_copy(d):
        return pltpu.make_async_copy(enc.at[0, :, pl.ds(rays_of(d), Q), :], xb.at[d], s_enc.at[d])

    enc_copy(0).start()
    load_mid = [
        pltpu.make_async_copy(wmid_h.at[0, :, pl.ds(h * FB, FB)], wmid.at[h], s_w.at[(1, 9)[h]]) for h in range(2)
    ]
    for h in range(2):
        load_mid[h].start()
    for d in range(1, XS):
        enc_copy(d).start()
    load_t = pltpu.make_async_copy(
        tgt.at[pl.ds(pl.multiple_of(x * Q + zj * RB, RB), RB), pl.ds(pl.multiple_of(zh * FB, FB), FB)], tb, s_w.at[2]
    )
    load_t.start()

    barrier = pltpu.get_barrier_semaphore()
    for k in range(1, YS):
        pl.semaphore_signal(barrier, inc=1, device_id=yd(k), device_id_type=MESH)
    pl.semaphore_signal(barrier, inc=1, device_id=other, device_id_type=MESH)
    each(0, ZP - 1, lambda i: pl.semaphore_signal(barrier, inc=1, device_id=zd(far_first(i, ZP)), device_id_type=MESH))
    each(1, G, lambda m: pl.semaphore_signal(barrier, inc=1, device_id=ahead(m), device_id_type=MESH))

    eye = lax.broadcasted_iota(jnp.int32, (Q, Q), 0) == lax.broadcasted_iota(jnp.int32, (Q, Q), 1)
    load_s.wait()
    sigma = wsig[...].astype(f32)
    for t in range(H // Q):
        wsr[t * Q:(t + 1) * Q, :] = column(sigma[:, t * Q:(t + 1) * Q]).astype(bf16)
    load_in.wait()

    load_d.wait()

    def density(d, _):
        enc_copy(d).wait()
        hp = jnp.dot(xb[d].reshape(S * Q, E), win[...], preferred_element_type=f32)
        h = jnp.maximum(hp, 0.0).astype(bf16)
        hid[d] = h
        lg = jnp.dot(h, wsr[...], preferred_element_type=f32)
        excl = jnp.zeros((1, Q), f32)
        for k in range(S):
            logit = jnp.sum(jnp.where(eye, lg[k * Q:(k + 1) * Q], 0.0), axis=0, keepdims=True)
            delta = dlt[0, k:k + 1, pl.ds(rays_of(d), Q)]
            tau = (jnp.maximum(logit, 0.0) + jnp.log1p(jnp.exp(-jnp.abs(logit)))) * delta
            comp[d, k:k + 1, :] = jnp.exp(-excl) * (1.0 - jnp.exp(-tau))
            excl = excl + tau
            comp[d, S + k:S + k + 1, :] = jnp.exp(-excl)
            comp[d, 2 * S + k:2 * S + k + 1, :] = delta / (1.0 + jnp.exp(-logit))
        tx_out[d] = stack([(0, excl)])
        return 0

    lax.fori_loop(0, XS, density, 0)

    def segments(d):
        hb = jnp.zeros((Q, H), f32)
        for k in range(S):
            wk = column(comp[d, k:k + 1, :])
            wrep[d, k] = wk
            hb = hb + wide(wk, H // Q) * hid[d, k * Q:(k + 1) * Q, :].astype(f32)
        hb_b = hb.astype(bf16)
        hbt[:, d * Q:(d + 1) * Q] = jnp.transpose(hb).astype(bf16)
        for h in range(2):
            sg_out[d, h] = jnp.dot(hb_b, wmid[h], preferred_element_type=f32).astype(bf16)

    pl.semaphore_wait(barrier, YS - 1 + 1 + ZP - 1 + G - 1)

    def tx(m):
        return remote(tx_out.at[m // 2], tx_in.at[m], tx_s.at[m], tx_r.at[m], ahead(m))

    def sg(m):
        return remote(sg_out.at[m // 2, (zh + m) % 2], sg_in.at[m], sg_s.at[m], sg_r.at[m], ahead(m))

    for m in (4, 5, 3, 7, 2, 6, 1):
        tx(m).start()
    tx_in[0] = tx_out[0]
    for h in range(2):
        load_mid[h].wait()
    for d in (2, 1):
        segments(d)
        sg(2 * d).start()
        sg(2 * d + 1).start()
    each(1, G, lambda m: tx(m).wait_recv())
    tz[0] = stack([(m, tx_in[m, 0:1, :]) for m in range(G)])

    def tz_copy(k):
        return remote(tz.at[0], tz.at[k], tz_s.at[k], tz_r.at[k], zd(k))

    each(0, ZP - 1, lambda i: tz_copy(far_first(i, ZP)).start())
    for d in (3, 0):
        segments(d)
        if d:
            sg(2 * d).start()
        sg(2 * d + 1).start()
    sg_in[0] = sg_out[0, zh]

    def turn(i, _):
        d, k = i // S, i % S
        t = jnp.transpose(xb[d, k].astype(f32)).astype(bf16)
        xt[d, :, pl.ds(pl.multiple_of(k * Q, Q), Q)] = t
        return 0

    lax.fori_loop(0, XS * S, turn, 0)
    load_o.wait()
    row = lax.broadcasted_iota(jnp.int32, (XS * ZS, XS * ZS), 0)
    place = lax.broadcasted_iota(jnp.int32, (XS * ZS, XS * ZS), 1)
    at_z = (z + ZS - 2 * (row // G)) % ZS + (row % 2) * (1 - 2 * zh)
    region = ((x + XS - row % G // 2) % XS) * ZS + at_z
    rank = jnp.sum(jnp.where(region == order[...], place, 0).astype(f32), axis=1, keepdims=True)

    each(1, ZP, lambda k: tz_copy(k).wait_recv())
    taus = tz[...].reshape(XS * ZS, Q)
    trans = []
    for m in range(G):
        front = rank < rank[m:m + 1]
        trans.append(jnp.exp(-jnp.sum(jnp.where(front, taus, 0.0), axis=0, keepdims=True)))
    for d in range(XS):
        tr_out[d] = stack([(0, trans[2 * d])])

    def tr(k):
        return remote(tr_out.at[k], tr_in.at[k], tr_s.at[k], tr_r.at[k], back(2 * k))

    for k in (2, 1, 3):
        tr(k).start()

    total = jnp.zeros((Q, FB), f32)
    for m in range(G):
        if m:
            sg(m).wait_recv()
        total = total + wide(column(trans[m]), FB // Q) * sg_in[m].astype(f32)
    zs[...] = total.astype(bf16)

    def zr_copy(k):
        src = zs.at[pl.ds(pl.multiple_of(((zj + k) % ZP) * RB, RB), RB), :]
        return remote(src, zr.at[k], zr_s.at[k], zr_r.at[k], zd(k))

    each(0, ZP - 1, lambda i: zr_copy(far_first(i, ZP)).start())
    zr[0] = zs[block, :]
    load_t.wait()
    each(1, ZP, lambda k: zr_copy(k).wait_recv())
    color = jnp.sum(zr[...].astype(f32), axis=0)
    err = color - tb[...].astype(f32)
    square = jnp.sum(err * err, axis=0, keepdims=True)
    square = square[:, :Q] + square[:, Q:]
    dc[0, zh, block, :] = err.astype(bf16)

    def za_copy(k):
        ref = dc.at[0, zh, block, :]
        return remote(ref, ref, za_s.at[k], za_r.at[k], zd(k))

    each(0, ZP - 1, lambda i: za_copy(far_first(i, ZP)).start())

    def za_wait(k):
        ref = dc.at[0, zh, pl.ds(pl.multiple_of(((zj + ZP - k) % ZP) * RB, RB), RB), :]
        remote(ref, ref, za_s.at[k], za_r.at[k], zd(k)).wait_recv()

    each(1, ZP, za_wait)

    def xa(m):
        half = (zh + m) % 2
        to = back(1) if m == 1 else back(m - m % 2)
        at = zh if m == 1 else half
        return remote(dc.at[0, at], dc.at[m // 2, at], xa_s.at[m], xa_r.at[m], to)

    def xa_wait(m):
        ref = dc.at[m // 2, (zh + m) % 2]
        remote(ref, ref, xa_s.at[m], xa_r.at[m], back(1)).wait_recv()

    for m in (1, 4, 2, 6):
        xa(m).start()

    grad = dc[0, zh].astype(f32)
    terms = []
    for m in range(G):
        prod = sg_in[m].astype(f32) * grad
        part = jnp.transpose(prod[:, :Q] + prod[:, Q:])
        terms.append(trans[m] * jnp.sum(part, axis=0, keepdims=True))
    uz[0, :G, :] = stack(list(enumerate(terms)))
    uz[0, G:, :] = stack([(0, square)])

    def uz_copy(k):
        return remote(uz.at[0], uz.at[k], uz_s.at[k], uz_r.at[k], zd(k))

    each(0, ZP - 1, lambda i: uz_copy(far_first(i, ZP)).start())
    xa_wait(1)
    for m in (5, 3, 7):
        xa(m).start()

    for k in range(1, XS):
        tr(k).wait_recv()
    tr_in[0] = tr_out[0]

    def cm(t):
        at = (zh + t) % 2
        return remote(cm_out.at[at], cm_in.at[at], c_s.at[(0, 3)[t]], c_r.at[(0, 3)[t]], other)

    def ym(t, k):
        at = (zh + t) % 2
        return remote(ym_out.at[at, (y + k) % YS], ym_in.at[at, k], ym_s.at[t, k], ym_r.at[t, k], yd(k))

    def mid_start(t):
        at = (zh + t) % 2
        for d in range(XS):
            if d:
                xa_wait(2 * d + t)
            shade = wide(column(tr_in[d, 0:1, :]), FB // Q)
            dsg[at, d * Q:(d + 1) * Q, :] = (shade * dc[d, at].astype(f32)).astype(bf16)
        mid = jnp.dot(hbt[...], dsg[at], preferred_element_type=f32)
        pmf[at] = mid.reshape(YS, 2, H // (2 * YS), FB)
        cm_out[at] = pmf[at, :, pl.ds(1 - c, 1)].reshape(YS, H // (2 * YS), FB).astype(bf16)
        cm(t).start()
        return lax.dot_general(dsg[at], wmid[at], (((1,), (1,)), ((), ())), preferred_element_type=f32)

    def mid_sum(t):
        at = (zh + t) % 2
        cm(t).wait_recv()
        own = pmf[at, :, pl.ds(c, 1)].reshape(YS, H // (2 * YS), FB) + cm_in[at].astype(f32)
        ym_own[at] = own
        ym_out[at] = own.astype(bf16)
        for k in (2, 1, 3):
            ym(t, k).start()

    gg[...] = mid_start(0).reshape(XS, Q, H)
    mid_sum(0)

    each(1, ZP, lambda k: uz_copy(k).wait_recv())
    us = uz[:, :G, :].reshape(XS * ZS, Q)
    squares = jnp.zeros((1, Q), f32)
    for k in range(ZP):
        squares = squares + uz[(zj + ZP - k) % ZP, G:G + 1, :]
    for m in range(G):
        behind = rank > rank[m:m + 1]
        gx_out[m] = stack([(0, -jnp.sum(jnp.where(behind, us, 0.0), axis=0, keepdims=True)), (1, squares)])

    def gx(m):
        return remote(gx_out.at[m], gx_in.at[m], gx_s.at[m], gx_r.at[m], back(m))

    each(1, G, lambda m: gx(m).start())
    gx_in[0] = gx_out[0]

    gg[...] += mid_start(1).reshape(XS, Q, H)
    mid_sum(1)

    def inner(d, _):
        g = gg[d]
        for k in range(S):
            prod = hid[d, k * Q:(k + 1) * Q, :].astype(f32) * g
            part = prod[:, :Q] + prod[:, Q:2 * Q] + prod[:, 2 * Q:3 * Q] + prod[:, 3 * Q:]
            vc[d, k:k + 1, :] = jnp.sum(jnp.transpose(part), axis=0, keepdims=True)
        return 0

    lax.fori_loop(0, XS, inner, 0)

    each(1, G, lambda m: gx(m).wait_recv())
    pif[...] = jnp.zeros_like(pif)
    lines = sigma

    def finish(d, sig):
        gtau = gx_in[2 * d, 0:1, :] + gx_in[2 * d + 1, 0:1, :]
        later = jnp.zeros((1, Q), f32)
        g = gg[d]
        for k in reversed(range(S)):
            v = vc[d, k:k + 1, :]
            dtau = comp[d, S + k:S + k + 1, :] * v - later + gtau
            later = later + comp[d, k:k + 1, :] * v
            dz = wide(column(dtau * comp[d, 2 * S + k:2 * S + k + 1, :]), H // Q)
            h = hid[d, k * Q:(k + 1) * Q, :].astype(f32)
            pre = wide(wrep[d, k], H // Q) * g + dz * lines
            dp[k * Q:(k + 1) * Q, :] = jnp.where(h > 0.0, pre, 0.0).astype(bf16)
            sig = sig + jnp.sum((h * dz).reshape(Q // 8, 8, H), axis=0)
        pif[...] += jnp.dot(xt[d], dp[...], preferred_element_type=f32).reshape(pif.shape)
        return sig

    sig = lax.fori_loop(0, XS, finish, jnp.zeros((8, H), f32))
    sig = jnp.sum(sig, axis=0, keepdims=True)
    ci_out[...] = pif[:, pl.ds(1 - c, 1)].reshape(YS, E // (2 * YS), H).astype(bf16)
    ci = remote(ci_out, ci_in, c_s.at[1], c_r.at[1], other)
    ci.start()
    squares = jnp.zeros((1, Q), f32)
    for q in range(XS):
        for h in range(2):
            squares = squares + gx_in[2 * ((q + XS - x) % XS) + (h + zh) % 2, 1:2, :]
    sb[...] = stack([(t, sig[:, t * Q:(t + 1) * Q]) for t in range(H // Q)] + [(H // Q, squares)])
    sc = remote(sb, sc_in, c_s.at[2], c_r.at[2], other)
    sc.start()
    ci.wait_recv()
    own = pif[:, pl.ds(c, 1)].reshape(YS, E // (2 * YS), H) + ci_in[...].astype(f32)
    yi_own[...] = own
    yi_out[...] = own.astype(bf16)

    def yi(k):
        return remote(yi_out.at[(y + k) % YS], yi_in.at[k], yi_s.at[k], yi_r.at[k], yd(k))

    for k in (2, 1, 3):
        yi(k).start()
    sc.wait_recv()
    sy_out[...] = sb[...] + sc_in[...]
    sy_in[0] = sy_out[...]

    def sy(k):
        return remote(sy_out, sy_in.at[k], sy_s.at[k], sy_r.at[k], yd(k))

    for k in (2, 1, 3):
        sy(k).start()

    for t in range(2):
        for k in range(1, YS):
            ym(t, k).wait_recv()
    for h in range(2):
        total = ym_own[h, y]
        for k in range(1, YS):
            total = total + ym_in[h, k].astype(f32)
        gm[0, :, h * FB:(h + 1) * FB] = total
    put_mid = pltpu.make_async_copy(gm, gm_o, s_w.at[6])
    put_mid.start()
    for k in range(1, YS):
        yi(k).wait_recv()
    total = yi_own[y]
    for k in range(1, YS):
        total = total + yi_in[k].astype(f32)
    gi[0] = total
    put_in = pltpu.make_async_copy(gi, gi_o, s_w.at[7])
    put_in.start()
    for k in range(1, YS):
        sy(k).wait_recv()
    total = jnp.zeros((8, Q), f32)
    for k in range(YS):
        total = total + sy_in[(y + YS - k) % YS]
    line = jnp.sum(jnp.where(lax.broadcasted_iota(jnp.int32, (8, Q), 0) == y, total, 0.0), axis=0, keepdims=True)
    gs[...] = jnp.where(c == 0, line[:, :Q // 2], line[:, Q // 2:])
    put_sig = pltpu.make_async_copy(gs, gs_o, s_w.at[8])
    put_sig.start()
    loss[0, 0] = jnp.sum(total[H // Q:H // Q + 1]) / (XS * Q * 2 * YS * F)

    put_mid.wait()
    put_in.wait()
    put_sig.wait()
    for k in range(1, XS):
        tr(k).wait_send()
        ym(0, k).wait_send()
        ym(1, k).wait_send()
        yi(k).wait_send()
        sy(k).wait_send()
    cm(0).wait_send()
    cm(1).wait_send()
    ci.wait_send()
    sc.wait_send()

    def sent_group(m):
        tx(m).wait_send()
        sg(m).wait_send()
        xa(m).wait_send()
        gx(m).wait_send()

    each(1, G, sent_group)

    def sent_z(k):
        tz_copy(k).wait_send()
        zr_copy(k).wait_send()
        za_copy(k).wait_send()
        uz_copy(k).wait_send()

    each(1, ZP, sent_z)


def settle(gi, gm, gs, loss, gi_o, gm_o, gs_o, loss_o):
    gi_o[...] = gi[...]
    gm_o[...] = gm[...]
    gs_o[...] = gs[...]
    loss_o[0, 0] = loss[0, 0]


def body(encoded, deltas, w_in, w_mid, w_sigma, order, target):
    hbm = pl.BlockSpec(memory_space=pl.ANY)
    vm = pl.BlockSpec(memory_space=pltpu.VMEM)
    dma = pltpu.SemaphoreType.DMA
    v = pltpu.VMEM
    hm, hi = H // (2 * YS), E // (2 * YS)
    scratch = [
        v((1, hi, H), f32), v((1, hm, F), f32), v((1, hm), f32),
        v((XS, S, Q, E), bf16), v((E, H), bf16), v((2, H, FB), bf16), v((RB, FB), bf16), v((H, Q), bf16),
        v((XS, S * Q, H), bf16), v((H, XS * Q), bf16), v((XS, E, S * Q), bf16), v((XS, S, Q, Q), f32), v((XS, 16, Q), f32),
        v((XS, 2, Q, FB), bf16), v((G, Q, FB), bf16), v((XS, 8, Q), f32), v((G, 8, Q), f32), v((ZP, 8, Q), f32),
        v((XS, 8, Q), f32), v((XS, 8, Q), f32),
        v((Q, FB), bf16), v((ZP, RB, FB), bf16), v((XS, 2, Q, FB), bf16), v((ZP, 16, Q), f32),
        v((G, 8, Q), f32), v((G, 8, Q), f32),
        v((2, XS * Q, FB), bf16), v((XS, Q, H), f32), v((XS, 8, Q), f32), v((2, YS, 2, hm, FB), f32),
        v((2, YS, hm, FB), bf16), v((2, YS, hm, FB), bf16), v((2, YS, hm, FB), f32), v((2, YS, hm, FB), bf16),
        v((2, YS, hm, FB), bf16),
        v((YS, 2, hi, H), f32),
        v((YS, hi, H), bf16), v((YS, hi, H), bf16), v((YS, hi, H), f32), v((YS, hi, H), bf16), v((YS, hi, H), bf16),
        v((8, Q), f32), v((8, Q), f32), v((8, Q), f32), v((YS, 8, Q), f32), v((S * Q, H), bf16),
        v((1, S, XS * Q), f32), v((1, H), bf16), v((1, XS * ZS), jnp.int32),
        dma((XS,)), dma((10,)), dma((G,)), dma((G,)), dma((G,)), dma((G,)), dma((ZP,)), dma((ZP,)),
        dma((XS,)), dma((XS,)), dma((ZP,)), dma((ZP,)), dma((ZP,)), dma((ZP,)),
        dma((G,)), dma((G,)), dma((ZP,)), dma((ZP,)), dma((G,)), dma((G,)), dma((4,)), dma((4,)),
        dma((2, YS)), dma((2, YS)), dma((YS,)), dma((YS,)), dma((YS,)), dma((YS,)),
    ]
    grad_in, grad_mid, grad_sigma, loss = pl.pallas_call(
        kernel,
        out_shape=(
            jax.ShapeDtypeStruct((1, hi, H), f32),
            jax.ShapeDtypeStruct((1, hm, F), f32),
            jax.ShapeDtypeStruct((1, hm), f32),
            jax.ShapeDtypeStruct((1, 1), f32),
        ),
        in_specs=[hbm] * 7,
        out_specs=(hbm, hbm, hbm, pl.BlockSpec(memory_space=pltpu.SMEM)),
        scratch_shapes=scratch,
        compiler_params=pltpu.CompilerParams(collective_id=0, has_side_effects=True, vmem_limit_bytes=60 << 20),
        name="field_step",
    )(encoded, deltas, w_in, w_mid, w_sigma, order, target)
    smem = pl.BlockSpec(memory_space=pltpu.SMEM)
    grad_in, grad_mid, grad_sigma, loss = pl.pallas_call(
        settle,
        out_shape=tuple(jax.ShapeDtypeStruct(a.shape, a.dtype) for a in (grad_in, grad_mid, grad_sigma, loss)),
        in_specs=[vm] * 3 + [smem],
        out_specs=(vm, vm, vm, smem),
        compiler_params=pltpu.CompilerParams(vmem_limit_bytes=60 << 20),
        name="settle",
    )(grad_in, grad_mid, grad_sigma, loss)
    return grad_in, grad_mid, grad_sigma, loss[0, 0]


def solution(mesh):
    in_specs = (
        P("depth", None, "rays", None),
        P("depth", None, "rays"),
        P("depth", None, None),
        P("depth", None, None),
        P("depth", None),
        P("rays", None),
        P("rays", None),
    )
    out_specs = (P("depth", "rays", None), P("depth", "rays", None), P("depth", "rays"), P())
    return jax.shard_map(body, mesh=mesh, in_specs=in_specs, out_specs=out_specs, check_vma=False)
```

```python
import functools

import jax
import jax.numpy as jnp
from jax import lax
from jax.experimental import pallas as pl
from jax.experimental.pallas import tpu as pltpu
from jax.sharding import PartitionSpec as P

MESH = pl.DeviceIdType.MESH
XS, ZS, YS = 4, 16, 4
ZP = ZS // 2
G = 2 * XS
S = 4
Q = 128
E, H, F = 256, 512, 512
FB = 256
HB = 256
RB = 16
bf16, f32 = jnp.bfloat16, jnp.float32


def coords():
    d = lax.axis_index("depth")
    r = lax.axis_index("rays")
    return d // ZS, d % ZS, r // 2, r % 2


def device(x, z, y, c):
    return (x * ZS + z, y * 2 + c)


def remote(src, dst, send, recv, to):
    return pltpu.make_async_remote_copy(
        src_ref=src, dst_ref=dst, send_sem=send, recv_sem=recv, device_id=to, device_id_type=MESH
    )


def column(row):
    return jnp.transpose(jnp.broadcast_to(row, (Q, Q)))


def wide(a, n):
    return jnp.concatenate([a] * n, axis=1)


def stack(rows):
    at = lax.broadcasted_iota(jnp.int32, (8, Q), 0)
    out = jnp.zeros((8, Q), f32)
    for i, row in rows:
        out = jnp.where(at == i, row, out)
    return out


def far_first(i, n):
    k = (i + 1) // 2
    return n // 2 + k * (2 * (i % 2) - 1)


def each(first, last, f):
    for i in range(first, last):
        f(i)


def kernel(
    enc, dlt_h, win_h, wmid_h, wsig_h, order_h, tgt,
    gi_o, gm_o, gs_o, loss,
    gi, gm, gs, xb, win, wmid, tb, wsr, hid, hbt, xt, wrep, comp,
    sg_out, sg_in, tx_out, tx_in, tz, tr_out, tr_in,
    zs, zr, dc, uz, gx_out, gx_in,
    dsg, gg, vc, pmf, cm_out, cm_in, ym_own, ym_out, ym_in,
    pif, ci_out, ci_in, yi_own, yi_out, yi_in, sb, sc_in, sy_out, sy_in, dp, dzc, dlt, wsig, order,
    s_enc, s_w, sg_s, sg_r, tx_s, tx_r, tz_s, tz_r, tr_s, tr_r, zr_s, zr_r, za_s, za_r,
    xa_s, xa_r, uz_s, uz_r, gx_s, gx_r, c_s, c_r, ym_s, ym_r, yi_s, yi_r, sy_s, sy_r,
):
    x, z, y, c = coords()
    xd = lambda k: device((x + k) % XS, z, y, c)
    zd = lambda k: device(x, (z + 2 * k) % ZS, y, c)
    yd = lambda k: device(x, z, (y + k) % YS, c)
    other = device(x, z, y, 1 - c)
    zj, zh = z // 2, z % 2
    pair = lambda e: z + e * (1 - 2 * zh)
    ahead = lambda m: device((x + m // 2) % XS, pair(m % 2), y, c)
    back = lambda m: device((x + XS - m // 2) % XS, pair(m % 2), y, c)
    block = pl.ds(pl.multiple_of(zj * RB, RB), RB)

    def rays_of(d):
        return pl.multiple_of(((x + d) % XS) * Q, Q)

    load_s = pltpu.make_async_copy(wsig_h, wsig, s_w.at[3])
    load_s.start()
    load_d = pltpu.make_async_copy(dlt_h, dlt, s_w.at[4])
    load_d.start()
    load_o = pltpu.make_async_copy(order_h, order, s_w.at[5])
    load_o.start()
    load_in = pltpu.make_async_copy(win_h.at[0], win, s_w.at[0])
    load_in.start()

    def rows_of(d):
        return pl.ds(d * Q if isinstance(d, int) else pl.multiple_of(d * Q, Q), Q)

    def enc_copy(d):
        return pltpu.make_async_copy(enc.at[0, :, pl.ds(rays_of(d), Q), :], xb.at[d], s_enc.at[d])

    enc_copy(0).start()
    load_mid = [
        pltpu.make_async_copy(wmid_h.at[0, :, pl.ds(h * FB, FB)], wmid.at[h], s_w.at[(1, 9)[h]]) for h in range(2)
    ]
    for h in range(2):
        load_mid[h].start()
    for d in range(1, XS):
        enc_copy(d).start()
    load_t = pltpu.make_async_copy(
        tgt.at[pl.ds(pl.multiple_of(x * Q + zj * RB, RB), RB), pl.ds(pl.multiple_of(zh * FB, FB), FB)], tb, s_w.at[2]
    )
    load_t.start()

    barrier = pltpu.get_barrier_semaphore()
    for k in range(1, YS):
        pl.semaphore_signal(barrier, inc=1, device_id=yd(k), device_id_type=MESH)
    pl.semaphore_signal(barrier, inc=1, device_id=other, device_id_type=MESH)
    each(0, ZP - 1, lambda i: pl.semaphore_signal(barrier, inc=1, device_id=zd(far_first(i, ZP)), device_id_type=MESH))
    each(1, G, lambda m: pl.semaphore_signal(barrier, inc=1, device_id=ahead(m), device_id_type=MESH))

    eye = lax.broadcasted_iota(jnp.int32, (Q, Q), 0) == lax.broadcasted_iota(jnp.int32, (Q, Q), 1)
    load_s.wait()
    sigma = wsig[...].astype(f32)
    for t in range(H // Q):
        wsr[t * Q:(t + 1) * Q, :] = column(sigma[:, t * Q:(t + 1) * Q]).astype(bf16)
    load_in.wait()

    load_d.wait()

    def density(d, _):
        enc_copy(d).wait()
        hp = jnp.dot(xb[d].reshape(S * Q, E), win[...], preferred_element_type=f32)
        h = jnp.maximum(hp, 0.0).astype(bf16)
        hid[d] = h
        lg = jnp.dot(h, wsr[...], preferred_element_type=f32)
        excl = jnp.zeros((1, Q), f32)
        for k in range(S):
            logit = jnp.sum(jnp.where(eye, lg[k * Q:(k + 1) * Q], 0.0), axis=0, keepdims=True)
            delta = dlt[0, k:k + 1, pl.ds(rays_of(d), Q)]
            tau = (jnp.maximum(logit, 0.0) + jnp.log1p(jnp.exp(-jnp.abs(logit)))) * delta
            comp[d, k:k + 1, :] = jnp.exp(-excl) * (1.0 - jnp.exp(-tau))
            excl = excl + tau
            comp[d, S + k:S + k + 1, :] = jnp.exp(-excl)
            comp[d, 2 * S + k:2 * S + k + 1, :] = delta / (1.0 + jnp.exp(-logit))
        tx_out[d] = stack([(0, excl)])
        return 0

    lax.fori_loop(0, XS, density, 0)

    def segments(d):
        hb = jnp.zeros((Q, H), f32)
        for k in range(S):
            wk = column(comp[d, k:k + 1, :])
            wrep[d, k] = wk
            hb = hb + wide(wk, H // Q) * hid[d, k * Q:(k + 1) * Q, :].astype(f32)
        hb_b = hb.astype(bf16)
        hbt[:, d * Q:(d + 1) * Q] = jnp.transpose(hb).astype(bf16)
        for h in range(2):
            sg_out[d, h] = jnp.dot(hb_b, wmid[h], preferred_element_type=f32).astype(bf16)

    pl.semaphore_wait(barrier, YS - 1 + 1 + ZP - 1 + G - 1)

    def tx(m):
        return remote(tx_out.at[m // 2], tx_in.at[m], tx_s.at[m], tx_r.at[m], ahead(m))

    def sg(m):
        return remote(sg_out.at[m // 2, (zh + m) % 2], sg_in.at[m], sg_s.at[m], sg_r.at[m], ahead(m))

    for m in (4, 5, 3, 7, 2, 6, 1):
        tx(m).start()
    tx_in[0] = tx_out[0]
    for h in range(2):
        load_mid[h].wait()
    for d in (2,):
        segments(d)
        sg(2 * d).start()
        sg(2 * d + 1).start()
    each(1, G, lambda m: tx(m).wait_recv())
    tz[0] = stack([(m, tx_in[m, 0:1, :]) for m in range(G)])

    def tz_copy(k):
        return remote(tz.at[0], tz.at[k], tz_s.at[k], tz_r.at[k], zd(k))

    each(0, ZP - 1, lambda i: tz_copy(far_first(i, ZP)).start())
    for d in (1, 3, 0):
        segments(d)
        if d:
            sg(2 * d).start()
        sg(2 * d + 1).start()
    sg_in[0] = sg_out[0, zh]

    def turn(i, _):
        d, k = i // S, i % S
        t = jnp.transpose(xb[d, k].astype(f32)).astype(bf16)
        xt[d, :, pl.ds(pl.multiple_of(k * Q, Q), Q)] = t
        return 0

    lax.fori_loop(0, XS * S, turn, 0)
    load_o.wait()
    row = lax.broadcasted_iota(jnp.int32, (XS * ZS, XS * ZS), 0)
    place = lax.broadcasted_iota(jnp.int32, (XS * ZS, XS * ZS), 1)
    at_z = (z + ZS - 2 * (row // G)) % ZS + (row % 2) * (1 - 2 * zh)
    region = ((x + XS - row % G // 2) % XS) * ZS + at_z
    rank = jnp.sum(jnp.where(region == order[...], place, 0).astype(f32), axis=1, keepdims=True)

    each(1, ZP, lambda k: tz_copy(k).wait_recv())
    taus = tz[...].reshape(XS * ZS, Q)
    trans = []
    for m in range(G):
        front = rank < rank[m:m + 1]
        trans.append(jnp.exp(-jnp.sum(jnp.where(front, taus, 0.0), axis=0, keepdims=True)))
    for d in range(XS):
        tr_out[d] = stack([(0, trans[2 * d])])

    def tr(k):
        return remote(tr_out.at[k], tr_in.at[k], tr_s.at[k], tr_r.at[k], back(2 * k))

    for k in (2, 1, 3):
        tr(k).start()

    total = jnp.zeros((Q, FB), f32)
    for m in range(G):
        if m:
            sg(m).wait_recv()
        total = total + wide(column(trans[m]), FB // Q) * sg_in[m].astype(f32)
    zs[...] = total.astype(bf16)

    def zr_copy(k):
        src = zs.at[pl.ds(pl.multiple_of(((zj + k) % ZP) * RB, RB), RB), :]
        return remote(src, zr.at[k], zr_s.at[k], zr_r.at[k], zd(k))

    each(0, ZP - 1, lambda i: zr_copy(far_first(i, ZP)).start())
    zr[0] = zs[block, :]
    load_t.wait()
    each(1, ZP, lambda k: zr_copy(k).wait_recv())
    color = jnp.sum(zr[...].astype(f32), axis=0)
    err = color - tb[...].astype(f32)
    square = jnp.sum(err * err, axis=0, keepdims=True)
    square = square[:, :Q] + square[:, Q:]
    dc[0, zh, block, :] = err.astype(bf16)

    def za_copy(k):
        ref = dc.at[0, zh, block, :]
        return remote(ref, ref, za_s.at[k], za_r.at[k], zd(k))

    each(0, ZP - 1, lambda i: za_copy(far_first(i, ZP)).start())

    def za_wait(k):
        ref = dc.at[0, zh, pl.ds(pl.multiple_of(((zj + ZP - k) % ZP) * RB, RB), RB), :]
        remote(ref, ref, za_s.at[k], za_r.at[k], zd(k)).wait_recv()

    each(1, ZP, za_wait)

    def xa(m):
        half = (zh + m) % 2
        to = back(1) if m == 1 else back(m - m % 2)
        at = zh if m == 1 else half
        return remote(dc.at[0, at], dc.at[m // 2, at], xa_s.at[m], xa_r.at[m], to)

    def xa_wait(m):
        ref = dc.at[m // 2, (zh + m) % 2]
        remote(ref, ref, xa_s.at[m], xa_r.at[m], back(1)).wait_recv()

    for m in (1, 4, 2, 6):
        xa(m).start()

    grad = dc[0, zh].astype(f32)
    terms = []
    for m in range(G):
        prod = sg_in[m].astype(f32) * grad
        part = jnp.transpose(prod[:, :Q] + prod[:, Q:])
        terms.append(trans[m] * jnp.sum(part, axis=0, keepdims=True))
    uz[0, :G, :] = stack(list(enumerate(terms)))
    uz[0, G:, :] = stack([(0, square)])

    def uz_copy(k):
        return remote(uz.at[0], uz.at[k], uz_s.at[k], uz_r.at[k], zd(k))

    each(0, ZP - 1, lambda i: uz_copy(far_first(i, ZP)).start())
    xa_wait(1)
    for m in (5, 3, 7):
        xa(m).start()

    for k in range(1, XS):
        tr(k).wait_recv()
    tr_in[0] = tr_out[0]

    def cm(t):
        at = (zh + t) % 2
        return remote(cm_out.at[at], cm_in.at[at], c_s.at[(0, 3)[t]], c_r.at[(0, 3)[t]], other)

    def ym(t, k):
        at = (zh + t) % 2
        return remote(ym_out.at[at, (y + k) % YS], ym_in.at[at, k], ym_s.at[t, k], ym_r.at[t, k], yd(k))

    def mid_start(t):
        at = (zh + t) % 2
        for d in range(XS):
            if d:
                xa_wait(2 * d + t)
            shade = wide(column(tr_in[d, 0:1, :]), FB // Q)
            dsg[at, d * Q:(d + 1) * Q, :] = (shade * dc[d, at].astype(f32)).astype(bf16)
        mid = jnp.dot(hbt[...], dsg[at], preferred_element_type=f32)
        pmf[at] = mid.reshape(YS, 2, H // (2 * YS), FB)
        cm_out[at] = pmf[at, :, pl.ds(1 - c, 1)].reshape(YS, H // (2 * YS), FB).astype(bf16)
        cm(t).start()
        return lax.dot_general(dsg[at], wmid[at], (((1,), (1,)), ((), ())), preferred_element_type=f32)

    def mid_sum(t):
        at = (zh + t) % 2
        cm(t).wait_recv()
        own = pmf[at, :, pl.ds(c, 1)].reshape(YS, H // (2 * YS), FB) + cm_in[at].astype(f32)
        ym_own[at] = own
        ym_out[at] = own.astype(bf16)
        for k in (2, 1, 3):
            ym(t, k).start()

    gg[...] = mid_start(0).reshape(XS, Q, H)
    mid_sum(0)

    each(1, ZP, lambda k: uz_copy(k).wait_recv())
    us = uz[:, :G, :].reshape(XS * ZS, Q)
    squares = jnp.zeros((1, Q), f32)
    for k in range(ZP):
        squares = squares + uz[(zj + ZP - k) % ZP, G:G + 1, :]
    for m in range(G):
        behind = rank > rank[m:m + 1]
        gx_out[m] = stack([(0, -jnp.sum(jnp.where(behind, us, 0.0), axis=0, keepdims=True)), (1, squares)])

    def gx(m):
        return remote(gx_out.at[m], gx_in.at[m], gx_s.at[m], gx_r.at[m], back(m))

    for m in (4, 5, 3, 7, 2, 6, 1):
        gx(m).start()
    gx_in[0] = gx_out[0]

    gg[...] += mid_start(1).reshape(XS, Q, H)
    mid_sum(1)

    def inner(d, _):
        g = gg[d]
        for k in range(S):
            prod = hid[d, k * Q:(k + 1) * Q, :].astype(f32) * g
            part = prod[:, :Q] + prod[:, Q:2 * Q] + prod[:, 2 * Q:3 * Q] + prod[:, 3 * Q:]
            vc[d, k:k + 1, :] = jnp.sum(jnp.transpose(part), axis=0, keepdims=True)
        return 0

    lax.fori_loop(0, XS, inner, 0)

    each(1, G, lambda m: gx(m).wait_recv())
    pif[...] = jnp.zeros_like(pif)

    def finish(half):
        cols = slice(half * HB, (half + 1) * HB)

        def step(d, _):
            if half == 0:
                gtau = gx_in[2 * d, 0:1, :] + gx_in[2 * d + 1, 0:1, :]
                later = jnp.zeros((1, Q), f32)
                for k in reversed(range(S)):
                    v = vc[d, k:k + 1, :]
                    dtau = comp[d, S + k:S + k + 1, :] * v - later + gtau
                    later = later + comp[d, k:k + 1, :] * v
                    dzc[d, k] = column(dtau * comp[d, 2 * S + k:2 * S + k + 1, :])
            for k in range(S):
                h = hid[d, k * Q:(k + 1) * Q, cols]
                pre = wide(wrep[d, k], HB // Q) * gg[d, :, cols] + wide(dzc[d, k], HB // Q) * sigma[:, cols]
                dp[k * Q:(k + 1) * Q, :] = jnp.where(h > 0, pre, 0.0).astype(bf16)
            pif[half] += jnp.dot(xt[d], dp[...], preferred_element_type=f32).reshape(YS, 2, E // (2 * YS), HB)
            return 0

        lax.fori_loop(0, XS, step, 0)
        ci_out[half] = pif[half, :, pl.ds(1 - c, 1)].reshape(YS, E // (2 * YS), HB).astype(bf16)
        ci(half).start()

    def ci(half):
        at = (1, 4)[half]
        return remote(ci_out.at[half], ci_in.at[half], c_s.at[at], c_r.at[at], other)

    def yi(half, k):
        return remote(
            yi_out.at[half, (y + k) % YS], yi_in.at[half, k], yi_s.at[half, k], yi_r.at[half, k], yd(k)
        )

    def in_sum(half):
        ci(half).wait_recv()
        own = pif[half, :, pl.ds(c, 1)].reshape(YS, E // (2 * YS), HB) + ci_in[half].astype(f32)
        yi_own[half] = own
        yi_out[half] = own.astype(bf16)
        for k in (2, 1, 3):
            yi(half, k).start()

    finish(0)
    finish(1)
    in_sum(0)

    def spread(d, sig):
        for k in range(S):
            prod = hid[d, k * Q:(k + 1) * Q, :].astype(f32) * wide(dzc[d, k], H // Q)
            sig = sig + jnp.sum(prod.reshape(Q // 8, 8, H), axis=0)
        return sig

    sig = jnp.sum(lax.fori_loop(0, XS, spread, jnp.zeros((8, H), f32)), axis=0, keepdims=True)
    squares = jnp.zeros((1, Q), f32)
    for q in range(XS):
        for h in range(2):
            squares = squares + gx_in[2 * ((q + XS - x) % XS) + (h + zh) % 2, 1:2, :]
    sb[...] = stack([(t, sig[:, t * Q:(t + 1) * Q]) for t in range(H // Q)] + [(H // Q, squares)])
    sc = remote(sb, sc_in, c_s.at[2], c_r.at[2], other)
    sc.start()
    in_sum(1)
    sc.wait_recv()
    sy_out[...] = sb[...] + sc_in[...]
    sy_in[0] = sy_out[...]

    def sy(k):
        return remote(sy_out, sy_in.at[k], sy_s.at[k], sy_r.at[k], yd(k))

    for k in (2, 1, 3):
        sy(k).start()

    for k in range(1, XS):
        tr(k).wait_send()
        ym(0, k).wait_send()
        ym(1, k).wait_send()
    cm(0).wait_send()
    cm(1).wait_send()
    ci(0).wait_send()
    ci(1).wait_send()
    sc.wait_send()

    def sent_group(m):
        tx(m).wait_send()
        sg(m).wait_send()
        xa(m).wait_send()
        gx(m).wait_send()

    each(1, G, sent_group)

    def sent_z(k):
        tz_copy(k).wait_send()
        zr_copy(k).wait_send()
        za_copy(k).wait_send()
        uz_copy(k).wait_send()

    each(1, ZP, sent_z)

    for t in range(2):
        for k in range(1, YS):
            ym(t, k).wait_recv()
    for h in range(2):
        total = ym_own[h, y]
        for k in range(1, YS):
            total = total + ym_in[h, k].astype(f32)
        gm[0, :, h * FB:(h + 1) * FB] = total
    put_mid = pltpu.make_async_copy(gm, gm_o, s_w.at[6])
    put_mid.start()
    for h in range(2):
        total = yi_own[h, y]
        for k in range(1, YS):
            yi(h, k).wait_recv()
            total = total + yi_in[h, k].astype(f32)
        gi[0, :, h * HB:(h + 1) * HB] = total
    put_in = pltpu.make_async_copy(gi, gi_o, s_w.at[7])
    put_in.start()
    for k in range(1, YS):
        sy(k).wait_recv()
    total = jnp.zeros((8, Q), f32)
    for k in range(YS):
        total = total + sy_in[(y + YS - k) % YS]
    line = jnp.sum(jnp.where(lax.broadcasted_iota(jnp.int32, (8, Q), 0) == y, total, 0.0), axis=0, keepdims=True)
    gs[...] = jnp.where(c == 0, line[:, :Q // 2], line[:, Q // 2:])
    put_sig = pltpu.make_async_copy(gs, gs_o, s_w.at[8])
    put_sig.start()
    loss[0, 0] = jnp.sum(total[H // Q:H // Q + 1]) / (XS * Q * 2 * YS * F)

    put_mid.wait()
    put_in.wait()
    put_sig.wait()
    for k in range(1, XS):
        yi(0, k).wait_send()
        yi(1, k).wait_send()
        sy(k).wait_send()


def settle(gi, gm, gs, loss, gi_o, gm_o, gs_o, loss_o):
    gi_o[...] = gi[...]
    gm_o[...] = gm[...]
    gs_o[...] = gs[...]
    loss_o[0, 0] = loss[0, 0]


def body(encoded, deltas, w_in, w_mid, w_sigma, order, target):
    hbm = pl.BlockSpec(memory_space=pl.ANY)
    vm = pl.BlockSpec(memory_space=pltpu.VMEM)
    dma = pltpu.SemaphoreType.DMA
    v = pltpu.VMEM
    hm, hi = H // (2 * YS), E // (2 * YS)
    scratch = [
        v((1, hi, H), f32), v((1, hm, F), f32), v((1, hm), f32),
        v((XS, S, Q, E), bf16), v((E, H), bf16), v((2, H, FB), bf16), v((RB, FB), bf16), v((H, Q), bf16),
        v((XS, S * Q, H), bf16), v((H, XS * Q), bf16), v((XS, E, S * Q), bf16), v((XS, S, Q, Q), f32), v((XS, 16, Q), f32),
        v((XS, 2, Q, FB), bf16), v((G, Q, FB), bf16), v((XS, 8, Q), f32), v((G, 8, Q), f32), v((ZP, 8, Q), f32),
        v((XS, 8, Q), f32), v((XS, 8, Q), f32),
        v((Q, FB), bf16), v((ZP, RB, FB), bf16), v((XS, 2, Q, FB), bf16), v((ZP, 16, Q), f32),
        v((G, 8, Q), f32), v((G, 8, Q), f32),
        v((2, XS * Q, FB), bf16), v((XS, Q, H), f32), v((XS, 8, Q), f32), v((2, YS, 2, hm, FB), f32),
        v((2, YS, hm, FB), bf16), v((2, YS, hm, FB), bf16), v((2, YS, hm, FB), f32), v((2, YS, hm, FB), bf16),
        v((2, YS, hm, FB), bf16),
        v((2, YS, 2, hi, HB), f32),
        v((2, YS, hi, HB), bf16), v((2, YS, hi, HB), bf16), v((2, YS, hi, HB), f32), v((2, YS, hi, HB), bf16),
        v((2, YS, hi, HB), bf16),
        v((8, Q), f32), v((8, Q), f32), v((8, Q), f32), v((YS, 8, Q), f32), v((S * Q, HB), bf16), v((XS, S, Q, Q), f32),
        v((1, S, XS * Q), f32), v((1, H), bf16), v((1, XS * ZS), jnp.int32),
        dma((XS,)), dma((10,)), dma((G,)), dma((G,)), dma((G,)), dma((G,)), dma((ZP,)), dma((ZP,)),
        dma((XS,)), dma((XS,)), dma((ZP,)), dma((ZP,)), dma((ZP,)), dma((ZP,)),
        dma((G,)), dma((G,)), dma((ZP,)), dma((ZP,)), dma((G,)), dma((G,)), dma((5,)), dma((5,)),
        dma((2, YS)), dma((2, YS)), dma((2, YS)), dma((2, YS)), dma((YS,)), dma((YS,)),
    ]
    grad_in, grad_mid, grad_sigma, loss = pl.pallas_call(
        kernel,
        out_shape=(
            jax.ShapeDtypeStruct((1, hi, H), f32),
            jax.ShapeDtypeStruct((1, hm, F), f32),
            jax.ShapeDtypeStruct((1, hm), f32),
            jax.ShapeDtypeStruct((1, 1), f32),
        ),
        in_specs=[hbm] * 7,
        out_specs=(hbm, hbm, hbm, pl.BlockSpec(memory_space=pltpu.SMEM)),
        scratch_shapes=scratch,
        compiler_params=pltpu.CompilerParams(collective_id=0, has_side_effects=True, vmem_limit_bytes=60 << 20),
        name="field_step",
    )(encoded, deltas, w_in, w_mid, w_sigma, order, target)
    smem = pl.BlockSpec(memory_space=pltpu.SMEM)
    grad_in, grad_mid, grad_sigma, loss = pl.pallas_call(
        settle,
        out_shape=tuple(jax.ShapeDtypeStruct(a.shape, a.dtype) for a in (grad_in, grad_mid, grad_sigma, loss)),
        in_specs=[vm] * 3 + [smem],
        out_specs=(vm, vm, vm, smem),
        compiler_params=pltpu.CompilerParams(vmem_limit_bytes=60 << 20),
        name="settle",
    )(grad_in, grad_mid, grad_sigma, loss)
    return grad_in, grad_mid, grad_sigma, loss[0, 0]


def solution(mesh):
    in_specs = (
        P("depth", None, "rays", None),
        P("depth", None, "rays"),
        P("depth", None, None),
        P("depth", None, None),
        P("depth", None),
        P("rays", None),
        P("rays", None),
    )
    out_specs = (P("depth", "rays", None), P("depth", "rays", None), P("depth", "rays"), P())
    return jax.shard_map(body, mesh=mesh, in_specs=in_specs, out_specs=out_specs, check_vma=False)
```

```python
import functools

import jax
import jax.numpy as jnp
from jax import lax
from jax.experimental import pallas as pl
from jax.experimental.pallas import tpu as pltpu
from jax.sharding import PartitionSpec as P

MESH = pl.DeviceIdType.MESH
XS, ZS, YS = 4, 16, 4
ZP = ZS // 2
G = 2 * XS
S = 4
Q = 128
E, H, F = 256, 512, 512
FB = 256
HB = 256
RB = 16
bf16, f32 = jnp.bfloat16, jnp.float32


def coords():
    d = lax.axis_index("depth")
    r = lax.axis_index("rays")
    return d // ZS, d % ZS, r // 2, r % 2


def device(x, z, y, c):
    return (x * ZS + z, y * 2 + c)


def remote(src, dst, send, recv, to):
    return pltpu.make_async_remote_copy(
        src_ref=src, dst_ref=dst, send_sem=send, recv_sem=recv, device_id=to, device_id_type=MESH
    )


def column(row):
    return jnp.transpose(jnp.broadcast_to(row, (Q, Q)))


def wide(a, n):
    return jnp.concatenate([a] * n, axis=1)


def stack(rows):
    at = lax.broadcasted_iota(jnp.int32, (8, Q), 0)
    out = jnp.zeros((8, Q), f32)
    for i, row in rows:
        out = jnp.where(at == i, row, out)
    return out


def far_first(i, n):
    k = (i + 1) // 2
    return n // 2 + k * (2 * (i % 2) - 1)


def each(first, last, f):
    for i in range(first, last):
        f(i)


def kernel(
    enc, dlt_h, win_h, wmid_h, wsig_h, order_h, tgt,
    gi_o, gm_o, gs_o, loss,
    gi, gm, gs, xb, win, wmid, tb, wsr, hid, hbt, xt, wrep, comp,
    sg_out, sg_in, tx_out, tx_in, tz, tr_out, tr_in,
    zs, zr, dc, uz, gx_out, gx_in,
    dsg, gg, vc, pmf, cm_out, cm_in, ym_own, ym_out, ym_in,
    pif, ci_out, ci_in, yi_own, yi_out, yi_in, sb, sc_in, sy_out, sy_in, dp, dzc, dlt, wsig, order,
    s_enc, s_w, sg_s, sg_r, tx_s, tx_r, tz_s, tz_r, tr_s, tr_r, zr_s, zr_r, za_s, za_r,
    xa_s, xa_r, uz_s, uz_r, gx_s, gx_r, c_s, c_r, ym_s, ym_r, yi_s, yi_r, sy_s, sy_r,
):
    x, z, y, c = coords()
    xd = lambda k: device((x + k) % XS, z, y, c)
    zd = lambda k: device(x, (z + 2 * k) % ZS, y, c)
    yd = lambda k: device(x, z, (y + k) % YS, c)
    other = device(x, z, y, 1 - c)
    zj, zh = z // 2, z % 2
    pair = lambda e: z + e * (1 - 2 * zh)
    ahead = lambda m: device((x + m // 2) % XS, pair(m % 2), y, c)
    back = lambda m: device((x + XS - m // 2) % XS, pair(m % 2), y, c)
    block = pl.ds(pl.multiple_of(zj * RB, RB), RB)

    def rays_of(d):
        return pl.multiple_of(((x + d) % XS) * Q, Q)

    load_s = pltpu.make_async_copy(wsig_h, wsig, s_w.at[3])
    load_s.start()
    load_d = pltpu.make_async_copy(dlt_h, dlt, s_w.at[4])
    load_d.start()
    load_o = pltpu.make_async_copy(order_h, order, s_w.at[5])
    load_o.start()
    load_in = pltpu.make_async_copy(win_h.at[0], win, s_w.at[0])
    load_in.start()

    def rows_of(d):
        return pl.ds(d * Q if isinstance(d, int) else pl.multiple_of(d * Q, Q), Q)

    def enc_copy(d):
        return pltpu.make_async_copy(enc.at[0, :, pl.ds(rays_of(d), Q), :], xb.at[d], s_enc.at[d])

    enc_copy(0).start()
    load_mid = [
        pltpu.make_async_copy(wmid_h.at[0, :, pl.ds(h * FB, FB)], wmid.at[h], s_w.at[(1, 9)[h]]) for h in range(2)
    ]
    for h in range(2):
        load_mid[h].start()
    for d in range(1, XS):
        enc_copy(d).start()
    load_t = pltpu.make_async_copy(
        tgt.at[pl.ds(pl.multiple_of(x * Q + zj * RB, RB), RB), pl.ds(pl.multiple_of(zh * FB, FB), FB)], tb, s_w.at[2]
    )
    load_t.start()

    barrier = pltpu.get_barrier_semaphore()
    for k in range(1, YS):
        pl.semaphore_signal(barrier, inc=1, device_id=yd(k), device_id_type=MESH)
    pl.semaphore_signal(barrier, inc=1, device_id=other, device_id_type=MESH)
    each(0, ZP - 1, lambda i: pl.semaphore_signal(barrier, inc=1, device_id=zd(far_first(i, ZP)), device_id_type=MESH))
    each(1, G, lambda m: pl.semaphore_signal(barrier, inc=1, device_id=ahead(m), device_id_type=MESH))

    eye = lax.broadcasted_iota(jnp.int32, (Q, Q), 0) == lax.broadcasted_iota(jnp.int32, (Q, Q), 1)
    load_s.wait()
    sigma = wsig[...].astype(f32)
    for t in range(H // Q):
        wsr[t * Q:(t + 1) * Q, :] = column(sigma[:, t * Q:(t + 1) * Q]).astype(bf16)
    load_in.wait()

    load_d.wait()

    def density(d, _):
        enc_copy(d).wait()
        hp = jnp.dot(xb[d].reshape(S * Q, E), win[...], preferred_element_type=f32)
        h = jnp.maximum(hp, 0.0).astype(bf16)
        hid[d] = h
        lg = jnp.dot(h, wsr[...], preferred_element_type=f32)
        excl = jnp.zeros((1, Q), f32)
        for k in range(S):
            logit = jnp.sum(jnp.where(eye, lg[k * Q:(k + 1) * Q], 0.0), axis=0, keepdims=True)
            delta = dlt[0, k:k + 1, pl.ds(rays_of(d), Q)]
            tau = (jnp.maximum(logit, 0.0) + jnp.log1p(jnp.exp(-jnp.abs(logit)))) * delta
            comp[d, k:k + 1, :] = jnp.exp(-excl) * (1.0 - jnp.exp(-tau))
            excl = excl + tau
            comp[d, S + k:S + k + 1, :] = jnp.exp(-excl)
            comp[d, 2 * S + k:2 * S + k + 1, :] = delta / (1.0 + jnp.exp(-logit))
        tx_out[d] = stack([(0, excl)])
        return 0

    lax.fori_loop(0, XS, density, 0)

    def segments(d):
        hb = jnp.zeros((Q, H), f32)
        for k in range(S):
            wk = column(comp[d, k:k + 1, :])
            wrep[d, k] = wk
            hb = hb + wide(wk, H // Q) * hid[d, k * Q:(k + 1) * Q, :].astype(f32)
        hb_b = hb.astype(bf16)
        hbt[:, d * Q:(d + 1) * Q] = jnp.transpose(hb).astype(bf16)
        for h in range(2):
            sg_out[d, h] = jnp.dot(hb_b, wmid[h], preferred_element_type=f32).astype(bf16)

    pl.semaphore_wait(barrier, YS - 1 + 1 + ZP - 1 + G - 1)

    def tx(m):
        return remote(tx_out.at[m // 2], tx_in.at[m], tx_s.at[m], tx_r.at[m], ahead(m))

    def sg(m):
        return remote(sg_out.at[m // 2, (zh + m) % 2], sg_in.at[m], sg_s.at[m], sg_r.at[m], ahead(m))

    for m in (4, 5, 3, 7, 2, 6, 1):
        tx(m).start()
    tx_in[0] = tx_out[0]
    for h in range(2):
        load_mid[h].wait()
    each(1, G, lambda m: tx(m).wait_recv())
    tz[0] = stack([(m, tx_in[m, 0:1, :]) for m in range(G)])

    def tz_copy(k):
        return remote(tz.at[0], tz.at[k], tz_s.at[k], tz_r.at[k], zd(k))

    each(0, ZP - 1, lambda i: tz_copy(far_first(i, ZP)).start())
    for d in (2, 1, 3, 0):
        segments(d)
        if d:
            sg(2 * d).start()
        sg(2 * d + 1).start()
    sg_in[0] = sg_out[0, zh]

    def turn(i, _):
        d, k = i // S, i % S
        t = jnp.transpose(xb[d, k].astype(f32)).astype(bf16)
        xt[d, :, pl.ds(pl.multiple_of(k * Q, Q), Q)] = t
        return 0

    lax.fori_loop(0, XS * S, turn, 0)
    load_o.wait()
    row = lax.broadcasted_iota(jnp.int32, (XS * ZS, XS * ZS), 0)
    place = lax.broadcasted_iota(jnp.int32, (XS * ZS, XS * ZS), 1)
    at_z = (z + ZS - 2 * (row // G)) % ZS + (row % 2) * (1 - 2 * zh)
    region = ((x + XS - row % G // 2) % XS) * ZS + at_z
    rank = jnp.sum(jnp.where(region == order[...], place, 0).astype(f32), axis=1, keepdims=True)

    each(1, ZP, lambda k: tz_copy(k).wait_recv())
    taus = tz[...].reshape(XS * ZS, Q)
    trans = []
    for m in range(G):
        front = rank < rank[m:m + 1]
        trans.append(jnp.exp(-jnp.sum(jnp.where(front, taus, 0.0), axis=0, keepdims=True)))
    for d in range(XS):
        tr_out[d] = stack([(0, trans[2 * d])])

    def tr(k):
        return remote(tr_out.at[k], tr_in.at[k], tr_s.at[k], tr_r.at[k], back(2 * k))

    for k in (2, 1, 3):
        tr(k).start()

    total = jnp.zeros((Q, FB), f32)
    for m in range(G):
        if m:
            sg(m).wait_recv()
        total = total + wide(column(trans[m]), FB // Q) * sg_in[m].astype(f32)
    zs[...] = total.astype(bf16)

    def zr_copy(k):
        src = zs.at[pl.ds(pl.multiple_of(((zj + k) % ZP) * RB, RB), RB), :]
        return remote(src, zr.at[k], zr_s.at[k], zr_r.at[k], zd(k))

    each(0, ZP - 1, lambda i: zr_copy(far_first(i, ZP)).start())
    zr[0] = zs[block, :]
    load_t.wait()
    each(1, ZP, lambda k: zr_copy(k).wait_recv())
    color = jnp.sum(zr[...].astype(f32), axis=0)
    err = color - tb[...].astype(f32)
    square = jnp.sum(err * err, axis=0, keepdims=True)
    square = square[:, :Q] + square[:, Q:]
    dc[0, zh, block, :] = err.astype(bf16)

    def za_copy(k):
        ref = dc.at[0, zh, block, :]
        return remote(ref, ref, za_s.at[k], za_r.at[k], zd(k))

    each(0, ZP - 1, lambda i: za_copy(far_first(i, ZP)).start())

    def za_wait(k):
        ref = dc.at[0, zh, pl.ds(pl.multiple_of(((zj + ZP - k) % ZP) * RB, RB), RB), :]
        remote(ref, ref, za_s.at[k], za_r.at[k], zd(k)).wait_recv()

    each(1, ZP, za_wait)

    def xa(m):
        half = (zh + m) % 2
        to = back(1) if m == 1 else back(m - m % 2)
        at = zh if m == 1 else half
        return remote(dc.at[0, at], dc.at[m // 2, at], xa_s.at[m], xa_r.at[m], to)

    def xa_wait(m):
        ref = dc.at[m // 2, (zh + m) % 2]
        remote(ref, ref, xa_s.at[m], xa_r.at[m], back(1)).wait_recv()

    for m in (1, 4, 2, 6):
        xa(m).start()

    grad = dc[0, zh].astype(f32)
    terms = []
    for m in range(G):
        prod = sg_in[m].astype(f32) * grad
        part = jnp.transpose(prod[:, :Q] + prod[:, Q:])
        terms.append(trans[m] * jnp.sum(part, axis=0, keepdims=True))
    uz[0, :G, :] = stack(list(enumerate(terms)))
    uz[0, G:, :] = stack([(0, square)])

    def uz_copy(k):
        return remote(uz.at[0], uz.at[k], uz_s.at[k], uz_r.at[k], zd(k))

    each(0, ZP - 1, lambda i: uz_copy(far_first(i, ZP)).start())
    xa_wait(1)
    for m in (5, 3, 7):
        xa(m).start()

    for k in range(1, XS):
        tr(k).wait_recv()
    tr_in[0] = tr_out[0]

    def cm(t):
        at = (zh + t) % 2
        return remote(cm_out.at[at], cm_in.at[at], c_s.at[(0, 3)[t]], c_r.at[(0, 3)[t]], other)

    def ym(t, k):
        at = (zh + t) % 2
        return remote(ym_out.at[at, (y + k) % YS], ym_in.at[at, k], ym_s.at[t, k], ym_r.at[t, k], yd(k))

    def mid_start(t):
        at = (zh + t) % 2
        for d in range(XS):
            if d:
                xa_wait(2 * d + t)
            shade = wide(column(tr_in[d, 0:1, :]), FB // Q)
            dsg[at, d * Q:(d + 1) * Q, :] = (shade * dc[d, at].astype(f32)).astype(bf16)
        mid = jnp.dot(hbt[...], dsg[at], preferred_element_type=f32)
        pmf[at] = mid.reshape(YS, 2, H // (2 * YS), FB)
        cm_out[at] = pmf[at, :, pl.ds(1 - c, 1)].reshape(YS, H // (2 * YS), FB).astype(bf16)
        cm(t).start()
        return lax.dot_general(dsg[at], wmid[at], (((1,), (1,)), ((), ())), preferred_element_type=f32)

    def mid_sum(t):
        at = (zh + t) % 2
        cm(t).wait_recv()
        own = pmf[at, :, pl.ds(c, 1)].reshape(YS, H // (2 * YS), FB) + cm_in[at].astype(f32)
        ym_own[at] = own
        ym_out[at] = own.astype(bf16)
        for k in (2, 1, 3):
            ym(t, k).start()

    gg[...] = mid_start(0).reshape(XS, Q, H)
    mid_sum(0)

    each(1, ZP, lambda k: uz_copy(k).wait_recv())
    us = uz[:, :G, :].reshape(XS * ZS, Q)
    squares = jnp.zeros((1, Q), f32)
    for k in range(ZP):
        squares = squares + uz[(zj + ZP - k) % ZP, G:G + 1, :]
    for m in range(G):
        behind = rank > rank[m:m + 1]
        gx_out[m] = stack([(0, -jnp.sum(jnp.where(behind, us, 0.0), axis=0, keepdims=True)), (1, squares)])

    def gx(m):
        return remote(gx_out.at[m], gx_in.at[m], gx_s.at[m], gx_r.at[m], back(m))

    for m in (4, 5, 3, 7, 2, 6, 1):
        gx(m).start()
    gx_in[0] = gx_out[0]

    gg[...] += mid_start(1).reshape(XS, Q, H)
    mid_sum(1)

    def inner(d, _):
        g = gg[d]
        for k in range(S):
            prod = hid[d, k * Q:(k + 1) * Q, :].astype(f32) * g
            part = prod[:, :Q] + prod[:, Q:2 * Q] + prod[:, 2 * Q:3 * Q] + prod[:, 3 * Q:]
            vc[d, k:k + 1, :] = jnp.sum(jnp.transpose(part), axis=0, keepdims=True)
        return 0

    lax.fori_loop(0, XS, inner, 0)

    each(1, G, lambda m: gx(m).wait_recv())
    pif[...] = jnp.zeros_like(pif)

    def finish(half):
        cols = slice(half * HB, (half + 1) * HB)

        def step(d, _):
            if half == 0:
                gtau = gx_in[2 * d, 0:1, :] + gx_in[2 * d + 1, 0:1, :]
                later = jnp.zeros((1, Q), f32)
                for k in reversed(range(S)):
                    v = vc[d, k:k + 1, :]
                    dtau = comp[d, S + k:S + k + 1, :] * v - later + gtau
                    later = later + comp[d, k:k + 1, :] * v
                    dzc[d, k] = column(dtau * comp[d, 2 * S + k:2 * S + k + 1, :])
            for k in range(S):
                h = hid[d, k * Q:(k + 1) * Q, cols]
                pre = wide(wrep[d, k], HB // Q) * gg[d, :, cols] + wide(dzc[d, k], HB // Q) * sigma[:, cols]
                dp[k * Q:(k + 1) * Q, :] = jnp.where(h > 0, pre, 0.0).astype(bf16)
            pif[half] += jnp.dot(xt[d], dp[...], preferred_element_type=f32).reshape(YS, 2, E // (2 * YS), HB)
            return 0

        lax.fori_loop(0, XS, step, 0)
        ci_out[half] = pif[half, :, pl.ds(1 - c, 1)].reshape(YS, E // (2 * YS), HB).astype(bf16)
        ci(half).start()

    def ci(half):
        at = (1, 4)[half]
        return remote(ci_out.at[half], ci_in.at[half], c_s.at[at], c_r.at[at], other)

    def yi(half, k):
        return remote(
            yi_out.at[half, (y + k) % YS], yi_in.at[half, k], yi_s.at[half, k], yi_r.at[half, k], yd(k)
        )

    def in_sum(half):
        ci(half).wait_recv()
        own = pif[half, :, pl.ds(c, 1)].reshape(YS, E // (2 * YS), HB) + ci_in[half].astype(f32)
        yi_own[half] = own
        yi_out[half] = own.astype(bf16)
        for k in (2, 1, 3):
            yi(half, k).start()

    finish(0)
    finish(1)
    in_sum(0)

    def spread(d, sig):
        for k in range(S):
            prod = hid[d, k * Q:(k + 1) * Q, :].astype(f32) * wide(dzc[d, k], H // Q)
            sig = sig + jnp.sum(prod.reshape(Q // 8, 8, H), axis=0)
        return sig

    sig = jnp.sum(lax.fori_loop(0, XS, spread, jnp.zeros((8, H), f32)), axis=0, keepdims=True)
    squares = jnp.zeros((1, Q), f32)
    for q in range(XS):
        for h in range(2):
            squares = squares + gx_in[2 * ((q + XS - x) % XS) + (h + zh) % 2, 1:2, :]
    sb[...] = stack([(t, sig[:, t * Q:(t + 1) * Q]) for t in range(H // Q)] + [(H // Q, squares)])
    sc = remote(sb, sc_in, c_s.at[2], c_r.at[2], other)
    sc.start()
    in_sum(1)
    sc.wait_recv()
    sy_out[...] = sb[...] + sc_in[...]
    sy_in[0] = sy_out[...]

    def sy(k):
        return remote(sy_out, sy_in.at[k], sy_s.at[k], sy_r.at[k], yd(k))

    for k in (2, 1, 3):
        sy(k).start()

    for k in range(1, XS):
        tr(k).wait_send()
        ym(0, k).wait_send()
        ym(1, k).wait_send()
    cm(0).wait_send()
    cm(1).wait_send()
    ci(0).wait_send()
    ci(1).wait_send()
    sc.wait_send()

    def sent_group(m):
        tx(m).wait_send()
        sg(m).wait_send()
        xa(m).wait_send()
        gx(m).wait_send()

    each(1, G, sent_group)

    def sent_z(k):
        tz_copy(k).wait_send()
        zr_copy(k).wait_send()
        za_copy(k).wait_send()
        uz_copy(k).wait_send()

    each(1, ZP, sent_z)

    for t in range(2):
        for k in range(1, YS):
            ym(t, k).wait_recv()
    for h in range(2):
        total = ym_own[h, y]
        for k in range(1, YS):
            total = total + ym_in[h, k].astype(f32)
        gm[0, :, h * FB:(h + 1) * FB] = total
    put_mid = pltpu.make_async_copy(gm, gm_o, s_w.at[6])
    put_mid.start()
    for h in range(2):
        total = yi_own[h, y]
        for k in range(1, YS):
            yi(h, k).wait_recv()
            total = total + yi_in[h, k].astype(f32)
        gi[0, :, h * HB:(h + 1) * HB] = total
    put_in = pltpu.make_async_copy(gi, gi_o, s_w.at[7])
    put_in.start()
    for k in range(1, YS):
        sy(k).wait_recv()
    total = jnp.zeros((8, Q), f32)
    for k in range(YS):
        total = total + sy_in[(y + YS - k) % YS]
    line = jnp.sum(jnp.where(lax.broadcasted_iota(jnp.int32, (8, Q), 0) == y, total, 0.0), axis=0, keepdims=True)
    gs[...] = jnp.where(c == 0, line[:, :Q // 2], line[:, Q // 2:])
    put_sig = pltpu.make_async_copy(gs, gs_o, s_w.at[8])
    put_sig.start()
    loss[0, 0] = jnp.sum(total[H // Q:H // Q + 1]) / (XS * Q * 2 * YS * F)

    put_mid.wait()
    put_in.wait()
    put_sig.wait()
    for k in range(1, XS):
        yi(0, k).wait_send()
        yi(1, k).wait_send()
        sy(k).wait_send()


def settle(gi, gm, gs, loss, gi_o, gm_o, gs_o, loss_o):
    gi_o[...] = gi[...]
    gm_o[...] = gm[...]
    gs_o[...] = gs[...]
    loss_o[0, 0] = loss[0, 0]


def body(encoded, deltas, w_in, w_mid, w_sigma, order, target):
    hbm = pl.BlockSpec(memory_space=pl.ANY)
    vm = pl.BlockSpec(memory_space=pltpu.VMEM)
    dma = pltpu.SemaphoreType.DMA
    v = pltpu.VMEM
    hm, hi = H // (2 * YS), E // (2 * YS)
    scratch = [
        v((1, hi, H), f32), v((1, hm, F), f32), v((1, hm), f32),
        v((XS, S, Q, E), bf16), v((E, H), bf16), v((2, H, FB), bf16), v((RB, FB), bf16), v((H, Q), bf16),
        v((XS, S * Q, H), bf16), v((H, XS * Q), bf16), v((XS, E, S * Q), bf16), v((XS, S, Q, Q), f32), v((XS, 16, Q), f32),
        v((XS, 2, Q, FB), bf16), v((G, Q, FB), bf16), v((XS, 8, Q), f32), v((G, 8, Q), f32), v((ZP, 8, Q), f32),
        v((XS, 8, Q), f32), v((XS, 8, Q), f32),
        v((Q, FB), bf16), v((ZP, RB, FB), bf16), v((XS, 2, Q, FB), bf16), v((ZP, 16, Q), f32),
        v((G, 8, Q), f32), v((G, 8, Q), f32),
        v((2, XS * Q, FB), bf16), v((XS, Q, H), f32), v((XS, 8, Q), f32), v((2, YS, 2, hm, FB), f32),
        v((2, YS, hm, FB), bf16), v((2, YS, hm, FB), bf16), v((2, YS, hm, FB), f32), v((2, YS, hm, FB), bf16),
        v((2, YS, hm, FB), bf16),
        v((2, YS, 2, hi, HB), f32),
        v((2, YS, hi, HB), bf16), v((2, YS, hi, HB), bf16), v((2, YS, hi, HB), f32), v((2, YS, hi, HB), bf16),
        v((2, YS, hi, HB), bf16),
        v((8, Q), f32), v((8, Q), f32), v((8, Q), f32), v((YS, 8, Q), f32), v((S * Q, HB), bf16), v((XS, S, Q, Q), f32),
        v((1, S, XS * Q), f32), v((1, H), bf16), v((1, XS * ZS), jnp.int32),
        dma((XS,)), dma((10,)), dma((G,)), dma((G,)), dma((G,)), dma((G,)), dma((ZP,)), dma((ZP,)),
        dma((XS,)), dma((XS,)), dma((ZP,)), dma((ZP,)), dma((ZP,)), dma((ZP,)),
        dma((G,)), dma((G,)), dma((ZP,)), dma((ZP,)), dma((G,)), dma((G,)), dma((5,)), dma((5,)),
        dma((2, YS)), dma((2, YS)), dma((2, YS)), dma((2, YS)), dma((YS,)), dma((YS,)),
    ]
    grad_in, grad_mid, grad_sigma, loss = pl.pallas_call(
        kernel,
        out_shape=(
            jax.ShapeDtypeStruct((1, hi, H), f32),
            jax.ShapeDtypeStruct((1, hm, F), f32),
            jax.ShapeDtypeStruct((1, hm), f32),
            jax.ShapeDtypeStruct((1, 1), f32),
        ),
        in_specs=[hbm] * 7,
        out_specs=(hbm, hbm, hbm, pl.BlockSpec(memory_space=pltpu.SMEM)),
        scratch_shapes=scratch,
        compiler_params=pltpu.CompilerParams(collective_id=0, has_side_effects=True, vmem_limit_bytes=60 << 20),
        name="field_step",
    )(encoded, deltas, w_in, w_mid, w_sigma, order, target)
    smem = pl.BlockSpec(memory_space=pltpu.SMEM)
    grad_in, grad_mid, grad_sigma, loss = pl.pallas_call(
        settle,
        out_shape=tuple(jax.ShapeDtypeStruct(a.shape, a.dtype) for a in (grad_in, grad_mid, grad_sigma, loss)),
        in_specs=[vm] * 3 + [smem],
        out_specs=(vm, vm, vm, smem),
        compiler_params=pltpu.CompilerParams(vmem_limit_bytes=60 << 20),
        name="settle",
    )(grad_in, grad_mid, grad_sigma, loss)
    return grad_in, grad_mid, grad_sigma, loss[0, 0]


def solution(mesh):
    in_specs = (
        P("depth", None, "rays", None),
        P("depth", None, "rays"),
        P("depth", None, None),
        P("depth", None, None),
        P("depth", None),
        P("rays", None),
        P("rays", None),
    )
    out_specs = (P("depth", "rays", None), P("depth", "rays", None), P("depth", "rays"), P())
    return jax.shard_map(body, mesh=mesh, in_specs=in_specs, out_specs=out_specs, check_vma=False)
```
